32 devices in a mesh: half: 4 (over x, core), wide: 8 (over z, y).
Axes of the slice: x: 2, y: 2, z: 4, core: 2. Of those that a mesh axis runs over, the one named last changes fastest.
Arguments:
- gains: float32 [4096, 4096], P(('half', 'wide')), parts along dimension 0, may hold values from -4 to 4
- response: bfloat16 [4096, 4096], P('wide', 'half'), parts along dimension 1, may hold values from -6 to 6
- student: bfloat16 [4096, 4096], P('wide', 'half'), parts along dimension 1, may hold values from 0.19921875 to 1
- blocks: bfloat16 [16, 256, 256], P('half'), parts along dimension 0, may hold values from -0.5 to 2.5, as said below
- order: int32 [4096], P('half'), parts along dimension 0, may hold values from 0 to 1023, each once
- lower: float32 [4096], P(('half', 'wide')), parts along dimension 0, may hold values from -1.2 to -0.4
- upper: float32 [4096], P(('half', 'wide')), parts along dimension 0, may hold values from 0.4 to 1.2
- lengths: float32 [4096], replicated, may hold values from 32 to 2048
- amplitude: float32 [4096], replicated, may hold values from 0.5 to 1.5
Outputs:
- tracked: float32 [4096, 4096], P(('half', 'wide')), parts along dimension 0
The draws below stay inside these ranges and needn't reach their ends.
There are 4 independent parts, one for each index of `half`. The reference program is written for one: setup_inputs(seed, part) draws one part's arguments, and reference() takes and returns one part's arrays. A program takes and returns all parts, laid end to end along the dimension named above; an argument that names none is the same for every part. Nothing has to cross between parts.
Inputs may be any that keep to these rules, and one draw needn't show every extreme that they name: `blocks`: each block is symmetric.
All inputs are finite; a program needn't handle non-finite values.
Results may differ from the reference program's by a relative error of at most 0.012.
The reference program's roundings to bfloat16 on the way (of `covar`, `packed` and `misfit`) count: a program that leaves them out, or rounds other values in their place, can miss the bound.
Values may be sent and summed in bfloat16 or wider, within the bound.
No kernel may reach another device: no remote copies, remote signals or barrier semaphores. Data moves between devices by JAX's collectives and lax.ppermute only.
A program may use at most 128 MiB of HBM per device.

```python
import math
import jax
import jax.numpy as jnp

E = 4096
BLOCK = 256
NBLK = 4
ITERS = 2
CH = 1024


def draw_blocks(key, part):
    noise_key = jax.random.fold_in(key, 11)
    noise = jax.random.normal(noise_key, (NBLK, BLOCK, BLOCK), jnp.float32)
    scale = 1.0 / BLOCK ** 0.5
    diag = 1.5
    sym = (noise + jnp.swapaxes(noise, 1, 2)) * (scale / 2.0 ** 0.5)
    sym = jnp.clip(sym, -0.5, 0.5)
    eye = jnp.eye(BLOCK, dtype=jnp.float32)[None, :, :]
    return (sym + diag * eye).astype(jnp.bfloat16)


def steps_of(own_key, dims, shards, least, top_value):
    factor_of = 1.0
    for position, shards_of in shards:
        draws = jax.random.uniform(jax.random.fold_in(jax.random.fold_in(own_key, 6), position), (shards_of,), jnp.float32, least / len(shards), top_value / len(shards))
        factor_of = factor_of * jnp.repeat(jnp.exp(draws), dims[position] // shards_of).reshape((-1,) + (1,) * (len(dims) - 1 - position))
    return factor_of


def scatter_about(key, shape, spread, limit, cuts=(), kind=jnp.bfloat16):
    factor_of = steps_of(key, shape, cuts, -0.22, 0.18) if cuts else 1.0
    drawn = jax.random.normal(key, shape, jnp.float32) * spread * factor_of
    return jnp.minimum(jnp.maximum(drawn, -limit), limit).astype(kind)


def setup_inputs(seed: int = 0, part: int = 0) -> dict:
    streams_of = jax.random.split(jax.random.key(seed), 10)
    part_splits = jax.random.split(jax.random.fold_in(streams_of[9], part), 10)
    return {
        "gains": scatter_about(part_splits[0], (CH, E), 0.8, 4.0, ((0, 8),), jnp.float32),
        "response": scatter_about(part_splits[1], (E, CH), 1.0, 6.0, ((0, 8),)),
        "student": jnp.clip(jnp.exp(math.log(1.0) - 1.6133518 * jax.random.uniform(part_splits[2], (E, CH), jnp.float32) ** steps_of(part_splits[2], (E, CH), ((0, 8),), -0.2, 0.2)), 0.19921875, 1.0).astype(jnp.bfloat16),
        "blocks": draw_blocks(jax.random.fold_in(jax.random.fold_in(streams_of[9], part), 71), part),
        "order": jax.random.permutation(part_splits[4], CH).astype(jnp.int32),
        "lower": jnp.clip(-1.2 + 0.800000042 * jax.random.uniform(part_splits[5], (CH,), jnp.float32) ** steps_of(part_splits[5], (CH,), ((0, 8),), -0.2, 0.2), -1.2, -0.4),
        "upper": jnp.clip(0.4 + 0.800000042 * jax.random.uniform(part_splits[6], (CH,), jnp.float32) ** steps_of(part_splits[6], (CH,), ((0, 8),), -0.2, 0.2), 0.4, 1.2),
        "lengths": jnp.clip(jnp.exp(jax.random.uniform(streams_of[7], (E,), jnp.float32, math.log(32.0), math.log(2048.0))), 32.0, 2048.0),
        "amplitude": jnp.clip(jnp.exp(jax.random.uniform(streams_of[8], (E,), jnp.float32, math.log(0.5), math.log(1.5))), 0.5, 1.5),
    }


def build_covar(lengths, amplitude):
    count = lengths.shape[0]
    rows = jnp.arange(count, dtype=jnp.int32)
    diff = (rows[:, None] - rows[None, :]).astype(lengths.dtype)
    left = lengths[:, None]
    right = lengths[None, :]
    denom = left * left + right * right
    vals = amplitude[:, None] * amplitude[None, :] * jnp.sqrt(2.0 * left * right / denom) * jnp.exp(-diff * diff / denom)
    return vals.astype(jnp.bfloat16)

def reference(gains, response, student, blocks, order, lower, upper, lengths, amplitude):
    covar = build_covar(lengths, amplitude)
    chans = gains.shape[0]
    nblk = blocks.shape[0]
    width = blocks.shape[1]
    inverse = jnp.zeros((chans,), jnp.int32).at[order].set(jnp.arange(chans, dtype=jnp.int32))
    resp_perm = jnp.take(response, order, axis=1).astype(jnp.float32)
    stud_perm = jnp.take(student, order, axis=1).astype(jnp.float32)
    current = gains
    for step in range(ITERS):
        packed = current.astype(jnp.bfloat16).T
        moved = jnp.take(packed, order, axis=1).reshape(packed.shape[0], nblk, width)
        product = jnp.einsum('rbi,bij->rbj', moved.astype(jnp.float32), blocks.astype(jnp.float32)).reshape(packed.shape[0], chans)
        permuted = stud_perm * (product - resp_perm)
        misfit = jnp.take(permuted, inverse, axis=1).astype(jnp.bfloat16).T
        smoothed = jnp.dot(misfit, covar, preferred_element_type=jnp.float32)
        current = jnp.clip(current - 0.02 * smoothed, lower[:, None], upper[:, None])
    return current
```

```python
import math
import jax
import jax.numpy as jnp
from jax import lax
from jax.experimental import pallas as pl
from jax.experimental.pallas import tpu as pltpu
from jax.sharding import PartitionSpec as P

ITERS = 2
LN2 = math.log(2.0)
F32 = jnp.float32
BF16 = jnp.bfloat16


def params(mib):
    return pltpu.CompilerParams(vmem_limit_bytes=mib * 1024 * 1024)


def cost(flops, moved, special=0):
    return pl.CostEstimate(flops=int(flops), bytes_accessed=int(moved), transcendentals=int(special))


def dot(a, b):
    return jnp.dot(a, b, preferred_element_type=F32)


def pack(me, gains, ndev, epd):
    chd = gains.shape[0]

    def body(me_ref, gains_ref, *outs):
        step = pl.program_id(0)
        for r in range(ndev):

            @pl.when(step == r)
            def _():
                outs[r][...] = gains_ref[...].astype(BF16)

    return pl.pallas_call(
        body,
        out_shape=[jax.ShapeDtypeStruct((chd, epd), BF16)] * ndev,
        grid_spec=pltpu.PrefetchScalarGridSpec(
            num_scalar_prefetch=1,
            grid=(ndev,),
            in_specs=[pl.BlockSpec((chd, epd), lambda r, me_ref: (0, me_ref[0] ^ r))],
            out_specs=[pl.BlockSpec((chd, epd), lambda r, me_ref: (0, 0))] * ndev,
        ),
        compiler_params=params(16),
        cost_estimate=cost(0, gains.size * 6),
        name="pack_gains",
    )(me, gains)


def flip(me, data, ndev):
    epd, chans = data.shape
    chd = chans // ndev

    def body(me_ref, data_ref, out_ref):
        out_ref[...] = data_ref[...].astype(F32).T.astype(BF16)

    return pl.pallas_call(
        body,
        out_shape=jax.ShapeDtypeStruct((chans, epd), BF16),
        grid_spec=pltpu.PrefetchScalarGridSpec(
            num_scalar_prefetch=1,
            grid=(ndev,),
            in_specs=[pl.BlockSpec((epd, chd), lambda r, me_ref: (0, me_ref[0] ^ r))],
            out_specs=pl.BlockSpec((chd, epd), lambda r, me_ref: (r, 0)),
        ),
        compiler_params=params(16),
        cost_estimate=cost(0, data.size * 4),
        name="flip",
    )(me, data)


def dense(me, blocks, order, ndev):
    nblk, width, _ = blocks.shape
    chans = nblk * width
    chd = chans // ndev

    def body(me_ref, blocks_ref, order_ref, out_ref, hot_ref, left_ref):
        row = lax.broadcasted_iota(jnp.int32, (chans, width), 0)
        chan = ((row // chd) ^ me_ref[0]) * chd + row % chd
        for b in range(nblk):
            hot = jnp.where(chan == order_ref[b : b + 1, :], 1.0, 0.0).astype(BF16)
            hot_ref[b] = hot
            left_ref[b] = dot(hot, blocks_ref[b]).astype(BF16)
        for r in range(ndev):
            rows = pl.ds(r * chd, chd)
            total = jnp.zeros((chd, chans), F32)
            for b in range(nblk):
                total += lax.dot_general(
                    left_ref[b, rows, :], hot_ref[b], (((1,), (1,)), ((), ())), preferred_element_type=F32
                )
            out_ref[rows, :] = total.astype(BF16)

    return pl.pallas_call(
        body,
        out_shape=jax.ShapeDtypeStruct((chans, chans), BF16),
        in_specs=[
            pl.BlockSpec(memory_space=pltpu.SMEM),
            pl.BlockSpec(memory_space=pltpu.VMEM),
            pl.BlockSpec(memory_space=pltpu.VMEM),
        ],
        out_specs=pl.BlockSpec(memory_space=pltpu.VMEM),
        scratch_shapes=[pltpu.VMEM((nblk, chans, width), BF16)] * 2,
        compiler_params=params(24),
        cost_estimate=cost(2 * chans * chans * (chans + width), chans * chans * 2),
        name="dense_blocks",
    )(me, blocks, order.reshape(nblk, width))


def covar(me, squares, scales, offsets, epd, rows=256):
    total = squares.shape[1]
    per = epd // rows
    first = offsets[0]

    def body(me_ref, sq_row, sc_row, sq_all, sc_all, out_ref, sq_col, sc_col):
        step = pl.program_id(0)
        device = me_ref[0] ^ (first + step // per)
        base = device * epd + (step % per) * rows
        for k in range(rows // 128):
            piece = pl.ds(k * 128, 128)
            sq_col[piece, :] = jnp.broadcast_to(sq_row[:, piece], (128, 128)).T
            sc_col[piece, :] = jnp.broadcast_to(sc_row[:, piece], (128, 128)).T
        lane = lax.broadcasted_iota(jnp.int32, (16, 128), 1)
        sub = lax.broadcasted_iota(jnp.int32, (16, 128), 0)
        away = (sub - lane).astype(F32)

        def group(g, _):
            at = pl.ds(pl.multiple_of(g * 16, 16), 16)
            sq_i = sq_col[at, :]
            sc_i = sc_col[at, :]
            start = away + (base + g * 16).astype(F32)
            for c in range(total // 128):
                cols = pl.ds(c * 128, 128)
                q = lax.rsqrt(sq_i + sq_all[:, cols])
                u = (start - float(c * 128)) * q
                out_ref[at, cols] = (q * jnp.exp2((sc_i + sc_all[:, cols]) - u * u)).astype(BF16)
            return 0

        lax.fori_loop(0, rows // 16, group, 0)

    def row_block(n, me_ref):
        return (0, (me_ref[0] ^ (first + n // per)) * per + n % per)

    count = len(offsets) * epd
    return pl.pallas_call(
        body,
        out_shape=jax.ShapeDtypeStruct((count, total), BF16),
        grid_spec=pltpu.PrefetchScalarGridSpec(
            num_scalar_prefetch=1,
            grid=(count // rows,),
            in_specs=[
                pl.BlockSpec((1, rows), row_block),
                pl.BlockSpec((1, rows), row_block),
                pl.BlockSpec((1, total), lambda n, me_ref: (0, 0)),
                pl.BlockSpec((1, total), lambda n, me_ref: (0, 0)),
            ],
            out_specs=pl.BlockSpec((rows, total), lambda n, me_ref: (n, 0)),
            scratch_shapes=[pltpu.VMEM((rows, 128), F32)] * 2,
        ),
        compiler_params=params(16),
        cost_estimate=cost(16 * count * total, count * total * 2, 2 * count * total),
        name="covar_rows",
    )(me, squares, scales, squares, scales)


def normal(weights, pieces, resp, stud):
    ndev = len(pieces)
    chd, epd = pieces[0].shape
    chans = ndev * chd
    steps = [r ^ (ndev // 2) for r in range(ndev)]

    def body(*refs):
        w_ref, resp_ref, stud_ref = refs[:3]
        ins = refs[3 : 3 + ndev]
        outs = refs[3 + ndev : 3 + 2 * ndev]
        got = refs[-1]
        step = pl.program_id(0)

        @pl.when(step == 0)
        def _():
            for r in range(ndev):
                got[pl.ds(r * chd, chd), :] = ins[r][...]

        out = stud_ref[...].astype(F32) * (dot(w_ref[...], got[...]) - resp_ref[...].astype(F32))
        out = out.astype(BF16)
        for k in range(ndev):

            @pl.when(step == k)
            def _():
                outs[steps[k]][...] = out

    def far_first(n):
        return (n ^ (ndev // 2), 0)

    whole = pl.BlockSpec((chd, epd), lambda n: (0, 0))
    return pl.pallas_call(
        body,
        out_shape=[jax.ShapeDtypeStruct((chd, epd), BF16)] * ndev,
        grid=(ndev,),
        in_specs=[
            pl.BlockSpec((chd, chans), far_first),
            pl.BlockSpec((chd, epd), far_first),
            pl.BlockSpec((chd, epd), far_first),
        ]
        + [whole] * ndev,
        out_specs=[whole] * ndev,
        scratch_shapes=[pltpu.VMEM((chans, epd), BF16)],
        compiler_params=params(24),
        cost_estimate=cost(2 * chans * chans * epd, chans * chans * 2 + chans * epd * 8),
        name="normal_step",
    )(weights, resp, stud, *pieces)


def smooth(pieces, rows, before):
    chd, epd = pieces[0].shape
    total = rows.shape[1]
    cnt = len(pieces)
    tile = epd

    def body(*refs):
        ins = refs[:cnt]
        rows_ref = refs[cnt]
        out_ref = refs[-1]
        acc = refs[cnt + 1][...] if before is not None else None
        for r in range(cnt):
            term = dot(ins[r][...], rows_ref[pl.ds(r * epd, epd), :])
            acc = term if acc is None else acc + term
        out_ref[...] = acc

    moving = pl.BlockSpec((chd, tile), lambda n: (0, n))
    more = [] if before is None else [before]
    return pl.pallas_call(
        body,
        out_shape=jax.ShapeDtypeStruct((chd, total), F32),
        grid=(total // tile,),
        in_specs=[pl.BlockSpec((chd, epd), lambda n: (0, 0))] * cnt
        + [pl.BlockSpec((cnt * epd, tile), lambda n: (0, n))]
        + [moving] * len(more),
        out_specs=moving,
        compiler_params=params(32),
        cost_estimate=cost(2 * chd * cnt * epd * total, cnt * epd * total * 2 + chd * total * 4),
        name="smooth_part",
    )(*pieces, rows, *more)


def update(me, pieces, rows, before, current, lower, upper, last):
    chd, epd = pieces[0].shape
    total = rows.shape[1]
    cnt = len(pieces)
    ndev = total // epd
    half = ndev // 2
    steps = list(range(ndev)) if last else [r ^ half for r in range(ndev)]

    def body(*refs):
        ins = refs[1 : 1 + cnt]
        rows_ref, before_ref, cur_ref, low_ref, high_ref, out_ref = refs[1 + cnt : 7 + cnt]
        acc = before_ref[...]
        for r in range(cnt):
            acc = acc + dot(ins[r][...], rows_ref[pl.ds(r * epd, epd), :])
        new = jnp.clip(cur_ref[...] - 0.02 * acc, low_ref[...], high_ref[...])
        out_ref[...] = new
        if not last:
            packed = new.astype(BF16)
            for k in range(ndev):

                @pl.when(pl.program_id(0) == k)
                def _():
                    refs[7 + cnt + steps[k]][...] = packed

    def column(n, me_ref):
        return (0, n if last else me_ref[0] ^ n ^ half)

    fixed = lambda n, me_ref: (0, 0)
    moving = pl.BlockSpec((chd, epd), column)
    whole = pl.BlockSpec((chd, epd), fixed)
    extra = 0 if last else ndev
    return pl.pallas_call(
        body,
        out_shape=[jax.ShapeDtypeStruct((chd, total), F32)] + [jax.ShapeDtypeStruct((chd, epd), BF16)] * extra,
        grid_spec=pltpu.PrefetchScalarGridSpec(
            num_scalar_prefetch=1,
            grid=(ndev,),
            in_specs=[whole] * cnt
            + [pl.BlockSpec((cnt * epd, epd), column), moving, moving]
            + [pl.BlockSpec((chd, 1), fixed)] * 2,
            out_specs=[moving] + [whole] * extra,
        ),
        compiler_params=params(32),
        cost_estimate=cost(2 * chd * cnt * epd * total, cnt * epd * total * 2 + chd * total * 14),
        name="update",
    )(me, *pieces, rows, before, current, lower, upper)


def swap(pieces):
    ndev = len(pieces)
    half = ndev // 2
    got = [pieces[0]] + [None] * (ndev - 1)
    for r in list(range(half, ndev)) + list(range(1, half)):
        got[r] = lax.ppermute(pieces[r], "wide", [(i, i ^ r) for i in range(ndev)])
    return got


def fast(gains, response, student, blocks, order, lower, upper, lengths, amplitude):
    ndev = lax.axis_size("wide")
    chd, epochs = gains.shape
    epd = epochs // ndev
    half = ndev // 2
    me = lax.axis_index("wide").astype(jnp.int32).reshape(1)
    low, high = lower[:, None], upper[:, None]

    packed = pack(me, gains, ndev, epd)
    got = swap(packed)
    weights = dense(me, blocks, order, ndev)
    resp = flip(me, response, ndev)
    stud = flip(me, student, ndev)
    squares = (lengths * lengths * LN2)[None, :]
    scales = jnp.log2(amplitude * jnp.sqrt(lengths * math.sqrt(2.0 * LN2)))[None, :]
    groups = [list(range(half)), list(range(half, half + half // 2)), list(range(half + half // 2, ndev))]
    rows = [covar(me, squares, scales, group, epd) for group in groups]
    current = gains
    for step in range(ITERS):
        misfit = swap(normal(weights, got, resp, stud))
        total = smooth([misfit[r] for r in groups[0]], rows[0], None)
        total = smooth([misfit[r] for r in groups[1]], rows[1], total)
        last = step == ITERS - 1
        current, *packed = update(me, [misfit[r] for r in groups[2]], rows[2], total, current, low, high, last)
        if not last:
            got = swap(packed)
    return current


def covar_stack(lengths, amplitude, span):
    total = lengths.shape[0]
    count = total // span
    rows = jnp.arange(total, dtype=jnp.int32)

    def one_block(index):
        start = index * span
        cols = start + jnp.arange(span, dtype=jnp.int32)
        diff = (rows[:, None] - cols[None, :]).astype(lengths.dtype)
        left = lengths[:, None]
        right = lax.dynamic_slice_in_dim(lengths, start, span, 0)[None, :]
        amp_right = lax.dynamic_slice_in_dim(amplitude, start, span, 0)[None, :]
        denom = left * left + right * right
        vals = (
            amplitude[:, None]
            * amp_right
            * jnp.sqrt(2.0 * left * right / denom)
            * jnp.exp(-diff * diff / denom)
        )
        return vals.astype(BF16)

    return lax.map(one_block, jnp.arange(count, dtype=jnp.int32))


def data_rows(packed, resp_perm, stud_perm, blocks, order, inverse):
    rows, chans = packed.shape
    nblk, width = (blocks.shape[0], blocks.shape[1])
    moved = jnp.take(packed, order, axis=1).reshape(rows, nblk, width)
    product = jnp.einsum("rbi,bij->rbj", moved, blocks, preferred_element_type=F32).reshape(rows, chans)
    permuted = stud_perm.astype(F32) * (product - resp_perm.astype(F32))
    return jnp.take(permuted, inverse, axis=1).astype(BF16)


def general(gains, response, student, blocks, order, lower, upper, lengths, amplitude):
    nwide = lax.axis_size("wide")
    chd, epochs = gains.shape
    epd = epochs // nwide
    chans = chd * nwide
    inverse = jnp.zeros((chans,), jnp.int32).at[order].set(jnp.arange(chans, dtype=jnp.int32))
    resp_perm = jnp.take(response, order, axis=1)
    stud_perm = jnp.take(student, order, axis=1)
    span = min(256, epochs)
    kernel_stack = covar_stack(lengths, amplitude, span)
    current = gains
    for step in range(ITERS):
        packed = current.astype(BF16).reshape(chd, nwide, epd)
        got = (
            lax.all_to_all(packed, "wide", split_axis=1, concat_axis=0, tiled=True)
            .reshape(chans, epd)
            .T
        )
        misfit_rows = data_rows(got, resp_perm, stud_perm, blocks, order, inverse)
        misfit = lax.all_to_all(
            misfit_rows.T.reshape(chans, 1, epd), "wide", split_axis=0, concat_axis=1, tiled=True
        ).reshape(chd, epochs)
        smoothed = jnp.einsum("ce,bes->cbs", misfit, kernel_stack, preferred_element_type=F32).reshape(
            chd, epochs
        )
        current = jnp.clip(current - 0.02 * smoothed, lower[:, None], upper[:, None])
    return current


def per_device(*args):
    ndev = lax.axis_size("wide")
    chd, epochs = args[0].shape
    fits = ndev >= 4 and ndev & (ndev - 1) == 0 and chd % 128 == 0 and (epochs // ndev) % 256 == 0
    return (fast if fits else general)(*args)


def solution(mesh):
    placed = (
        P(("half", "wide"), None),
        P("wide", "half"),
        P("wide", "half"),
        P("half", None, None),
        P("half"),
        P(("half", "wide")),
        P(("half", "wide")),
        P(),
        P(),
    )
    return jax.shard_map(
        per_device, mesh=mesh, in_specs=placed, out_specs=P(("half", "wide"), None), check_vma=False
    )
```

```python
import math
import jax
import jax.numpy as jnp
from jax import lax
from jax.experimental import pallas as pl
from jax.experimental.pallas import tpu as pltpu
from jax.sharding import PartitionSpec as P

ITERS = 2
LN2 = math.log(2.0)
F32 = jnp.float32
BF16 = jnp.bfloat16


def params(mib=8):
    return pltpu.CompilerParams(vmem_limit_bytes=mib * 1024 * 1024)


CHEAP = pl.CostEstimate(flops=1, bytes_accessed=1, transcendentals=0)
SMEM = pl.BlockSpec(memory_space=pltpu.SMEM)
VMEM = pl.BlockSpec(memory_space=pltpu.VMEM)
ANY = pl.BlockSpec(memory_space=pl.ANY)


def dot(a, b):
    return jnp.dot(a, b, preferred_element_type=F32)


def column(row):
    n = row.shape[1]
    return jnp.broadcast_to(row, (n, n)).T[:, :1]


def pack(me, gains, ndev, epd):
    chd, total = gains.shape
    half = ndev // 2

    def body(me_ref, gains_ref, *refs):
        outs, kept, sems = refs[:ndev], refs[ndev], refs[ndev + 1]
        order = [r ^ half for r in range(ndev)]

        def copy(r):
            cols = pl.ds(pl.multiple_of((me_ref[0] ^ r) * epd, epd), epd)
            return pltpu.make_async_copy(gains_ref.at[:, cols], kept.at[:, cols], sems.at[r])

        for r in order:
            copy(r).start()
        for r in order:
            copy(r).wait()
            cols = pl.ds(pl.multiple_of((me_ref[0] ^ r) * epd, epd), epd)
            outs[r][...] = kept[:, cols].astype(BF16)

    return pl.pallas_call(
        body,
        out_shape=[jax.ShapeDtypeStruct((chd, epd), BF16)] * ndev + [pltpu.VMEM((chd, total), F32)],
        in_specs=[SMEM, ANY],
        out_specs=[VMEM] * (ndev + 1),
        scratch_shapes=[pltpu.SemaphoreType.DMA((ndev,))],
        compiler_params=params(),
        cost_estimate=CHEAP,
        name="pack_gains",
    )(me, gains)


def flip(me, data, ndev):
    epd, chans = data.shape
    chd = chans // ndev

    def body(me_ref, data_ref, out_ref):
        for r in range(ndev):
            cols = pl.ds(pl.multiple_of((me_ref[0] ^ r) * chd, chd), chd)
            out_ref[pl.ds(r * chd, chd), :] = data_ref[:, cols].astype(F32).T.astype(BF16)

    return pl.pallas_call(
        body,
        out_shape=pltpu.VMEM((chans, epd), BF16),
        in_specs=[SMEM, VMEM],
        out_specs=VMEM,
        compiler_params=params(),
        cost_estimate=CHEAP,
        name="flip",
    )(me, data)


def dense(me, blocks, order, ndev):
    nblk, width, _ = blocks.shape
    chans = nblk * width
    chd = chans // ndev

    def body(me_ref, blocks_ref, order_ref, out_ref, hot_ref, left_ref):
        row = lax.broadcasted_iota(jnp.int32, (chans, width), 0)
        chan = ((row // chd) ^ me_ref[0]) * chd + row % chd
        for b in range(nblk):
            hot = jnp.where(chan == order_ref[:, pl.ds(b * width, width)], 1.0, 0.0).astype(BF16)
            hot_ref[b] = hot
            left_ref[b] = dot(hot, blocks_ref[b]).astype(BF16)
        for r in range(ndev):
            rows = pl.ds(r * chd, chd)
            total = jnp.zeros((chd, chans), F32)
            for b in range(nblk):
                total += lax.dot_general(
                    left_ref[b, rows, :], hot_ref[b], (((1,), (1,)), ((), ())), preferred_element_type=F32
                )
            out_ref[rows, :] = total.astype(BF16)

    return pl.pallas_call(
        body,
        out_shape=pltpu.VMEM((chans, chans), BF16),
        in_specs=[SMEM, VMEM, VMEM],
        out_specs=VMEM,
        scratch_shapes=[pltpu.VMEM((nblk, chans, width), BF16)] * 2,
        compiler_params=params(),
        cost_estimate=CHEAP,
        name="dense_blocks",
    )(me, blocks, order[None, :])


def covar(me, squares, scales, offsets, epd):
    total = squares.shape[1]
    per = epd // 128
    first = offsets[0]
    count = len(offsets) * epd

    def body(me_ref, sq_all, sc_all, out_ref, sq_col, sc_col):
        lane = lax.broadcasted_iota(jnp.int32, (16, 128), 1)
        sub = lax.broadcasted_iota(jnp.int32, (16, 128), 0)
        away = (sub - lane).astype(F32)

        def block(n, _):
            base = (me_ref[0] ^ (first + n // per)) * epd + (n % per) * 128
            span = pl.ds(pl.multiple_of(base, 128), 128)
            sq_col[...] = jnp.broadcast_to(sq_all[:, span], (128, 128)).T
            sc_col[...] = jnp.broadcast_to(sc_all[:, span], (128, 128)).T

            def group(g, _):
                part = pl.ds(pl.multiple_of(g * 16, 16), 16)
                at = pl.ds(pl.multiple_of(n * 128 + g * 16, 16), 16)
                sq_i = sq_col[part, :]
                sc_i = sc_col[part, :]
                start = away + (base + g * 16).astype(F32)
                for c in range(total // 128):
                    cols = pl.ds(c * 128, 128)
                    q = lax.rsqrt(sq_i + sq_all[:, cols])
                    u = (start - float(c * 128)) * q
                    out_ref[at, cols] = (q * jnp.exp2((sc_i + sc_all[:, cols]) - u * u)).astype(BF16)
                return 0

            return lax.fori_loop(0, 8, group, 0)

        lax.fori_loop(0, count // 128, block, 0)

    return pl.pallas_call(
        body,
        out_shape=pltpu.VMEM((count, total), BF16),
        in_specs=[SMEM, VMEM, VMEM],
        out_specs=VMEM,
        scratch_shapes=[pltpu.VMEM((128, 128), F32)] * 2,
        compiler_params=params(),
        cost_estimate=CHEAP,
        name="covar_rows",
    )(me, squares, scales)


def normal(weights, pieces, resp, stud):
    ndev = len(pieces)
    chd, epd = pieces[0].shape
    chans = ndev * chd
    half = ndev // 2

    def body(*refs):
        w_ref, resp_ref, stud_ref = refs[:3]
        ins = refs[3 : 3 + ndev]
        outs = refs[3 + ndev : 3 + 2 * ndev]
        got = refs[-1]
        for r in range(ndev):
            got[pl.ds(r * chd, chd), :] = ins[r][...]
        for r in [k ^ half for k in range(ndev)]:
            rows = pl.ds(r * chd, chd)
            product = dot(w_ref[rows, :], got[...])
            outs[r][...] = (stud_ref[rows, :].astype(F32) * (product - resp_ref[rows, :].astype(F32))).astype(BF16)

    return pl.pallas_call(
        body,
        out_shape=[jax.ShapeDtypeStruct((chd, epd), BF16)] * ndev,
        in_specs=[VMEM] * (3 + ndev),
        out_specs=[VMEM] * ndev,
        scratch_shapes=[pltpu.VMEM((chans, epd), BF16)],
        compiler_params=params(),
        cost_estimate=CHEAP,
        name="normal_step",
    )(weights, resp, stud, *pieces)


def smooth(pieces, rows, before):
    chd, epd = pieces[0].shape
    total = rows.shape[1]
    cnt = len(pieces)

    def body(*refs):
        ins = refs[:cnt]
        rows_ref = refs[cnt]
        out_ref = refs[-1]
        left = jnp.concatenate([ref[...] for ref in ins], axis=1)

        def tile(n, _):
            cols = pl.ds(pl.multiple_of(n * epd, epd), epd)
            acc = dot(left, rows_ref[:, cols])
            out_ref[:, cols] = acc if before is None else acc + refs[cnt + 1][:, cols]
            return 0

        lax.fori_loop(0, total // epd, tile, 0)

    more = [] if before is None else [before]
    return pl.pallas_call(
        body,
        out_shape=pltpu.VMEM((chd, total), F32),
        in_specs=[VMEM] * (cnt + 1 + len(more)),
        out_specs=VMEM,
        compiler_params=params(),
        cost_estimate=CHEAP,
        name="smooth_part",
    )(*pieces, rows, *more)


def update(me, pieces, rows, before, current, lower, upper, last):
    chd, epd = pieces[0].shape
    total = rows.shape[1]
    cnt = len(pieces)
    ndev = total // epd
    half = ndev // 2

    def body(*refs):
        me_ref = refs[0]
        ins = refs[1 : 1 + cnt]
        rows_ref, before_ref, cur_ref, low_ref, high_ref, out_ref = refs[1 + cnt : 7 + cnt]
        left = jnp.concatenate([ref[...] for ref in ins], axis=1)
        low, high = column(low_ref[...]), column(high_ref[...])
        copies = []
        for r in [k ^ half for k in range(ndev)]:
            cols = pl.ds(pl.multiple_of((me_ref[0] ^ r) * epd, epd), epd)
            acc = before_ref[:, cols] + dot(left, rows_ref[:, cols])
            new = jnp.clip(cur_ref[:, cols] - 0.02 * acc, low, high)
            if last:
                stage, sems = refs[-2:]
                stage[:, cols] = new
                copies.append(pltpu.make_async_copy(stage.at[:, cols], out_ref.at[:, cols], sems.at[r]))
                copies[-1].start()
            else:
                out_ref[:, cols] = new
                refs[7 + cnt + r][...] = new.astype(BF16)
        for copy in copies:
            copy.wait()

    if last:
        shapes, specs = [jax.ShapeDtypeStruct((chd, total), F32)], [ANY]
        scratch = [pltpu.VMEM((chd, total), F32), pltpu.SemaphoreType.DMA((ndev,))]
    else:
        shapes = [pltpu.VMEM((chd, total), F32)] + [jax.ShapeDtypeStruct((chd, epd), BF16)] * ndev
        specs, scratch = [VMEM] * (1 + ndev), []
    return pl.pallas_call(
        body,
        out_shape=shapes,
        in_specs=[SMEM] + [VMEM] * (cnt + 5),
        out_specs=specs,
        scratch_shapes=scratch,
        compiler_params=params(),
        cost_estimate=CHEAP,
        name="update",
    )(me, *pieces, rows, before, current, lower, upper)


def swap(pieces):
    ndev = len(pieces)
    half = ndev // 2
    got = [pieces[0]] + [None] * (ndev - 1)
    for r in list(range(half, ndev)) + list(range(1, half)):
        got[r] = lax.ppermute(pieces[r], "wide", [(i, i ^ r) for i in range(ndev)])
    return got


def fast(gains, response, student, blocks, order, lower, upper, lengths, amplitude):
    ndev = lax.axis_size("wide")
    chd, epochs = gains.shape
    epd = epochs // ndev
    half = ndev // 2
    me = lax.axis_index("wide").astype(jnp.int32).reshape(1)
    low, high = lower[None, :], upper[None, :]

    *packed, current = pack(me, gains, ndev, epd)
    got = swap(packed)
    weights = dense(me, blocks, order, ndev)
    resp = flip(me, response, ndev)
    stud = flip(me, student, ndev)
    squares = (lengths * lengths * LN2)[None, :]
    scales = jnp.log2(amplitude * jnp.sqrt(lengths * math.sqrt(2.0 * LN2)))[None, :]
    groups = [list(range(half)), list(range(half, half + half // 2)), list(range(half + half // 2, ndev))]
    rows = [covar(me, squares, scales, group, epd) for group in groups]
    got, rows = lax.optimization_barrier((got, rows))
    for step in range(ITERS):
        misfit = swap(normal(weights, got, resp, stud))
        total = smooth([misfit[r] for r in groups[0]], rows[0], None)
        total = smooth([misfit[r] for r in groups[1]], rows[1], total)
        last = step == ITERS - 1
        current, *packed = update(me, [misfit[r] for r in groups[2]], rows[2], total, current, low, high, last)
        if not last:
            got = swap(packed)
    return current


def covar_stack(lengths, amplitude, span):
    total = lengths.shape[0]
    count = total // span
    rows = jnp.arange(total, dtype=jnp.int32)

    def one_block(index):
        start = index * span
        cols = start + jnp.arange(span, dtype=jnp.int32)
        diff = (rows[:, None] - cols[None, :]).astype(lengths.dtype)
        left = lengths[:, None]
        right = lax.dynamic_slice_in_dim(lengths, start, span, 0)[None, :]
        amp_right = lax.dynamic_slice_in_dim(amplitude, start, span, 0)[None, :]
        denom = left * left + right * right
        vals = (
            amplitude[:, None]
            * amp_right
            * jnp.sqrt(2.0 * left * right / denom)
            * jnp.exp(-diff * diff / denom)
        )
        return vals.astype(BF16)

    return lax.map(one_block, jnp.arange(count, dtype=jnp.int32))


def data_rows(packed, resp_perm, stud_perm, blocks, order, inverse):
    rows, chans = packed.shape
    nblk, width = (blocks.shape[0], blocks.shape[1])
    moved = jnp.take(packed, order, axis=1).reshape(rows, nblk, width)
    product = jnp.einsum("rbi,bij->rbj", moved, blocks, preferred_element_type=F32).reshape(rows, chans)
    permuted = stud_perm.astype(F32) * (product - resp_perm.astype(F32))
    return jnp.take(permuted, inverse, axis=1).astype(BF16)


def general(gains, response, student, blocks, order, lower, upper, lengths, amplitude):
    nwide = lax.axis_size("wide")
    chd, epochs = gains.shape
    epd = epochs // nwide
    chans = chd * nwide
    inverse = jnp.zeros((chans,), jnp.int32).at[order].set(jnp.arange(chans, dtype=jnp.int32))
    resp_perm = jnp.take(response, order, axis=1)
    stud_perm = jnp.take(student, order, axis=1)
    span = min(256, epochs)
    kernel_stack = covar_stack(lengths, amplitude, span)
    current = gains
    for step in range(ITERS):
        packed = current.astype(BF16).reshape(chd, nwide, epd)
        got = (
            lax.all_to_all(packed, "wide", split_axis=1, concat_axis=0, tiled=True)
            .reshape(chans, epd)
            .T
        )
        misfit_rows = data_rows(got, resp_perm, stud_perm, blocks, order, inverse)
        misfit = lax.all_to_all(
            misfit_rows.T.reshape(chans, 1, epd), "wide", split_axis=0, concat_axis=1, tiled=True
        ).reshape(chd, epochs)
        smoothed = jnp.einsum("ce,bes->cbs", misfit, kernel_stack, preferred_element_type=F32).reshape(
            chd, epochs
        )
        current = jnp.clip(current - 0.02 * smoothed, lower[:, None], upper[:, None])
    return current


def per_device(*args):
    ndev = lax.axis_size("wide")
    chd, epochs = args[0].shape
    fits = ndev >= 4 and ndev & (ndev - 1) == 0 and chd % 128 == 0 and (epochs // ndev) % 256 == 0
    return (fast if fits else general)(*args)


def solution(mesh):
    placed = (
        P(("half", "wide"), None),
        P("wide", "half"),
        P("wide", "half"),
        P("half", None, None),
        P("half"),
        P(("half", "wide")),
        P(("half", "wide")),
        P(),
        P(),
    )
    return jax.shard_map(
        per_device, mesh=mesh, in_specs=placed, out_specs=P(("half", "wide"), None), check_vma=False
    )
```

```python
import math
import jax
import jax.numpy as jnp
from jax import lax
from jax.experimental import pallas as pl
from jax.experimental.pallas import tpu as pltpu
from jax.sharding import PartitionSpec as P

ITERS = 2
LN2 = math.log(2.0)
F32 = jnp.float32
BF16 = jnp.bfloat16


def params(mib=8):
    return pltpu.CompilerParams(vmem_limit_bytes=mib * 1024 * 1024)


CHEAP = pl.CostEstimate(flops=1, bytes_accessed=1, transcendentals=0)
SMEM = pl.BlockSpec(memory_space=pltpu.SMEM)
VMEM = pl.BlockSpec(memory_space=pltpu.VMEM)
HBM = pl.BlockSpec(memory_space=pltpu.HBM)


def dot(a, b):
    return jnp.dot(a, b, preferred_element_type=F32)


def column(row):
    n = row.shape[1]
    return jnp.broadcast_to(row, (n, n)).T[:, :1]


def send_order(ndev):
    half = ndev // 2
    return [half, *range(1, half), *range(half + 1, ndev), 0]


def pack(me, gains, ndev, epd):
    chd, total = gains.shape
    order = send_order(ndev)

    def body(me_ref, gains_ref, *refs):
        outs, kept, sems = refs[:ndev], refs[ndev], refs[ndev + 1]

        def copy(r):
            theirs = pl.ds(pl.multiple_of((me_ref[0] ^ r) * epd, epd), epd)
            return pltpu.make_async_copy(gains_ref.at[:, theirs], kept.at[:, pl.ds(r * epd, epd)], sems.at[r])

        for r in order:
            copy(r).start()
        for r in order:
            copy(r).wait()
            outs[r][...] = kept[:, pl.ds(r * epd, epd)].astype(BF16)

    return pl.pallas_call(
        body,
        out_shape=[jax.ShapeDtypeStruct((chd, epd), BF16)] * ndev + [pltpu.VMEM((chd, total), F32)],
        in_specs=[SMEM, HBM],
        out_specs=[VMEM] * (ndev + 1),
        scratch_shapes=[pltpu.SemaphoreType.DMA((ndev,))],
        compiler_params=params(),
        cost_estimate=CHEAP,
        name="pack_gains",
    )(me, gains)


def flip(me, data, ndev):
    epd, chans = data.shape
    chd = chans // ndev

    def body(me_ref, data_ref, out_ref):
        for r in range(ndev):
            cols = pl.ds(pl.multiple_of((me_ref[0] ^ r) * chd, chd), chd)
            out_ref[pl.ds(r * chd, chd), :] = data_ref[:, cols].astype(F32).T.astype(BF16)

    return pl.pallas_call(
        body,
        out_shape=pltpu.VMEM((chans, epd), BF16),
        in_specs=[SMEM, VMEM],
        out_specs=VMEM,
        compiler_params=params(),
        cost_estimate=CHEAP,
        name="flip",
    )(me, data)


def dense(me, blocks, order, ndev):
    nblk, width, _ = blocks.shape
    chans = nblk * width
    chd = chans // ndev

    def body(me_ref, blocks_ref, order_ref, out_ref, left_ref, hot_ref):
        def channels(dim, shape):
            at = lax.broadcasted_iota(jnp.int32, shape, dim)
            return (((at // chd) ^ me_ref[0]) * chd + at % chd).astype(F32)

        down = channels(0, (chans, width))
        along = channels(1, (width, chans))
        for b in range(nblk):
            span = pl.ds(b * width, width)
            names = order_ref[:, span].astype(F32)
            hot = jnp.where(down == names, 1.0, 0.0).astype(BF16)
            left_ref[:, span] = dot(hot, blocks_ref[b]).astype(BF16)
            hot_ref[span, :] = jnp.where(along == column(names), 1.0, 0.0).astype(BF16)
        for r in range(0, ndev, 2):
            rows = pl.ds(r * chd, 2 * chd)
            out_ref[rows, :] = dot(left_ref[rows, :], hot_ref[...]).astype(BF16)

    return pl.pallas_call(
        body,
        out_shape=pltpu.VMEM((chans, chans), BF16),
        in_specs=[SMEM, VMEM, VMEM],
        out_specs=VMEM,
        scratch_shapes=[pltpu.VMEM((chans, chans), BF16)] * 2,
        compiler_params=params(),
        cost_estimate=CHEAP,
        name="dense_blocks",
    )(me, blocks, order[None, :])


def covar_tiles(me_ref, sq_all, sc_all, sq_col, sc_col, offset, k, others, epd, store):
    group = 32
    lane = lax.broadcasted_iota(jnp.int32, (group, 128), 1)
    sub = lax.broadcasted_iota(jnp.int32, (group, 128), 0)
    away = (sub - lane).astype(F32)
    base = (me_ref[0] ^ offset) * epd + k * 128
    span = pl.ds(pl.multiple_of(base, 128), 128)
    sq_col[...] = jnp.broadcast_to(sq_all[:, span], (128, 128)).T
    sc_col[...] = jnp.broadcast_to(sc_all[:, span], (128, 128)).T
    for r in others:
        first = (me_ref[0] ^ r) * epd
        apart = (base - first).astype(F32)
        for c in range(0, epd, 128):
            cols = pl.ds(pl.multiple_of(first + c, 128), 128)
            sq_j, sc_j = sq_all[:, cols], sc_all[:, cols]
            parts = []
            for g in range(0, 128, group):
                rows = pl.ds(g, group)
                q = lax.rsqrt(sq_col[rows, :] + sq_j)
                u = (away + (apart + float(g - c))) * q
                parts.append((q * jnp.exp2((sc_col[rows, :] + sc_j) - u * u)).astype(BF16))
            store(r, c, jnp.concatenate(parts, axis=0))


def covar_own(me, squares, scales, offsets, epd):
    per = epd // 128
    first = offsets[0]
    count = len(offsets) * epd

    def body(me_ref, sq_all, sc_all, out_ref, sq_col, sc_col):
        for n, offset in enumerate(offsets):

            def block(k, _):
                mine = pl.ds(pl.multiple_of(n * epd + k * 128, 128), 128)

                def store(r, c, tile):
                    theirs = pl.ds((r - first) * epd + c, 128)
                    out_ref[mine, theirs] = tile
                    if r != offset:
                        out_ref[theirs, mine] = tile.T

                covar_tiles(me_ref, sq_all, sc_all, sq_col, sc_col, offset, k, offsets[n:], epd, store)
                return 0

            lax.fori_loop(0, per, block, 0)

    return pl.pallas_call(
        body,
        out_shape=pltpu.VMEM((count, count), BF16),
        in_specs=[SMEM, VMEM, VMEM],
        out_specs=VMEM,
        scratch_shapes=[pltpu.VMEM((128, 128), F32)] * 2,
        compiler_params=params(),
        cost_estimate=CHEAP,
        name="covar_own",
    )(me, squares, scales)


def covar_cross(me, squares, scales, near, far, epd):
    per = epd // 128
    shape = (len(near) * epd, len(far) * epd)

    def body(me_ref, sq_all, sc_all, out_ref, flip_ref, sq_col, sc_col):
        def block(n, _):
            mine = pl.ds(pl.multiple_of(n * 128, 128), 128)

            def store(r, c, tile):
                theirs = pl.ds((r - far[0]) * epd + c, 128)
                out_ref[mine, theirs] = tile
                flip_ref[theirs, mine] = tile.T

            covar_tiles(me_ref, sq_all, sc_all, sq_col, sc_col, near[0] + n // per, n % per, far, epd, store)
            return 0

        lax.fori_loop(0, shape[0] // 128, block, 0)

    return pl.pallas_call(
        body,
        out_shape=[pltpu.VMEM(shape, BF16), pltpu.VMEM(shape[::-1], BF16)],
        in_specs=[SMEM, VMEM, VMEM],
        out_specs=[VMEM] * 2,
        scratch_shapes=[pltpu.VMEM((128, 128), F32)] * 2,
        compiler_params=params(),
        cost_estimate=CHEAP,
        name="covar_cross",
    )(me, squares, scales)


def normal(weights, pieces, resp, stud):
    ndev = len(pieces)
    chd, epd = pieces[0].shape
    chans = ndev * chd

    def body(w_ref, resp_ref, stud_ref, *refs):
        ins, outs, got = refs[:ndev], refs[ndev:-1], refs[-1]
        for r in range(ndev):
            got[pl.ds(r * chd, chd), :] = ins[r][...]
        for r in send_order(ndev):
            rows = pl.ds(r * chd, chd)
            product = dot(w_ref[rows, :], got[...])
            outs[r][...] = (stud_ref[rows, :].astype(F32) * (product - resp_ref[rows, :].astype(F32))).astype(BF16)

    return pl.pallas_call(
        body,
        out_shape=[jax.ShapeDtypeStruct((chd, epd), BF16)] * ndev,
        in_specs=[VMEM] * (3 + ndev),
        out_specs=[VMEM] * ndev,
        scratch_shapes=[pltpu.VMEM((chans, epd), BF16)],
        compiler_params=params(),
        cost_estimate=CHEAP,
        name="normal_step",
    )(weights, resp, stud, *pieces)


def partial(groups, before):
    chd, epd = groups[0][0][0].shape
    span = groups[0][1][0].shape[1]
    blocks = len(groups[0][1])
    args = [array for pieces, rows, _ in groups for array in [*pieces, *rows]]
    more = [] if before is None else [before]

    def body(*refs):
        out_ref, given = refs[-1], iter(refs)
        terms = []
        for pieces, rows, at in groups:
            left = jnp.concatenate([next(given)[...] for _ in pieces], axis=1)
            terms.append((left, [next(given) for _ in rows], pl.ds(at, len(pieces) * epd)))
        for b in range(blocks):
            for c in range(0, span, epd):
                cols = pl.ds(b * span + c, epd)
                acc = None if before is None else refs[len(args)][:, cols]
                for left, rows_refs, at in terms:
                    term = dot(left, rows_refs[b][at, pl.ds(c, epd)])
                    acc = term if acc is None else acc + term
                out_ref[:, cols] = acc

    return pl.pallas_call(
        body,
        out_shape=pltpu.VMEM((chd, blocks * span), F32),
        in_specs=[VMEM] * (len(args) + len(more)),
        out_specs=VMEM,
        compiler_params=params(),
        cost_estimate=CHEAP,
        name="smooth_part",
    )(*args, *more)


def update(me, pieces, rows, at, before, current, lower, upper, last):
    chd, epd = pieces[0].shape
    cnt, blocks = len(pieces), len(rows)
    span = rows[0].shape[1]
    total = blocks * span
    ndev = total // epd

    def body(*refs):
        me_ref, ins, rows_refs = refs[0], refs[1 : 1 + cnt], refs[1 + cnt : 1 + cnt + blocks]
        before_ref, cur_ref, low_ref, high_ref, out_ref = refs[1 + cnt + blocks : 6 + cnt + blocks]
        left = jnp.concatenate([ref[...] for ref in ins], axis=1)
        low, high = column(low_ref[...]), column(high_ref[...])
        copies = []
        for r in send_order(ndev):
            cols = pl.ds(r * epd, epd)
            block, c = divmod(r * epd, span)
            acc = before_ref[:, cols] + dot(left, rows_refs[block][pl.ds(at, cnt * epd), pl.ds(c, epd)])
            new = jnp.clip(cur_ref[:, cols] - 0.02 * acc, low, high)
            if last:
                stage, sems = refs[-2:]
                stage[:, cols] = new
                theirs = pl.ds(pl.multiple_of((me_ref[0] ^ r) * epd, epd), epd)
                copies.append(pltpu.make_async_copy(stage.at[:, cols], out_ref.at[:, theirs], sems.at[r]))
                copies[-1].start()
            else:
                out_ref[:, cols] = new
                refs[6 + cnt + blocks + r][...] = new.astype(BF16)
        for copy in copies:
            copy.wait()

    if last:
        shapes, specs = [jax.ShapeDtypeStruct((chd, total), F32)], [HBM]
        scratch = [pltpu.VMEM((chd, total), F32), pltpu.SemaphoreType.DMA((ndev,))]
    else:
        shapes = [pltpu.VMEM((chd, total), F32)] + [jax.ShapeDtypeStruct((chd, epd), BF16)] * ndev
        specs, scratch = [VMEM] * (1 + ndev), []
    return pl.pallas_call(
        body,
        out_shape=shapes,
        in_specs=[SMEM] + [VMEM] * (cnt + blocks + 4),
        out_specs=specs,
        scratch_shapes=scratch,
        compiler_params=params(),
        cost_estimate=CHEAP,
        name="update",
    )(me, *pieces, *rows, before, current, lower, upper)


def swap(pieces):
    ndev = len(pieces)
    got = list(pieces)
    for r in send_order(ndev)[:-1]:
        got[r] = lax.ppermute(pieces[r], "wide", [(i, i ^ r) for i in range(ndev)])
    return got


def fast(gains, response, student, blocks, order, lower, upper, lengths, amplitude):
    ndev = lax.axis_size("wide")
    epd = gains.shape[1] // ndev
    half = ndev // 2
    near, far = list(range(half)), list(range(half, ndev))
    me = lax.axis_index("wide").astype(jnp.int32).reshape(1)
    low, high = lower[None, :], upper[None, :]

    *packed, current = pack(me, gains, ndev, epd)
    got = swap(packed)
    weights = dense(me, blocks, order, ndev)
    resp = flip(me, response, ndev)
    stud = flip(me, student, ndev)
    squares = (lengths * lengths * LN2)[None, :]
    scales = jnp.log2(amplitude * jnp.sqrt(lengths * math.sqrt(2.0 * LN2)))[None, :]
    near_far, far_near = covar_cross(me, squares, scales, near, far, epd)
    near_near = covar_own(me, squares, scales, near, epd)
    got, near_far, far_near, near_near = lax.optimization_barrier((got, near_far, far_near, near_near))
    far_far = covar_own(me, squares, scales, far, epd)
    near_rows, far_rows = [near_near, near_far], [far_near, far_far]
    late = 1
    for step in range(ITERS):
        misfit = swap(normal(weights, got, resp, stud))
        total = partial([(misfit[:1], near_rows, 0), (misfit[half : half + 1], far_rows, 0)], None)
        total = partial([(misfit[1:half], near_rows, epd)], total)
        total = partial([(misfit[half + 1 : ndev - late], far_rows, epd)], total)
        last = step == ITERS - 1
        current, *packed = update(
            me, misfit[ndev - late :], far_rows, (half - late) * epd, total, current, low, high, last
        )
        if not last:
            got = swap(packed)
    return current


def covar_stack(lengths, amplitude, span):
    total = lengths.shape[0]
    count = total // span
    rows = jnp.arange(total, dtype=jnp.int32)

    def one_block(index):
        start = index * span
        cols = start + jnp.arange(span, dtype=jnp.int32)
        diff = (rows[:, None] - cols[None, :]).astype(lengths.dtype)
        left = lengths[:, None]
        right = lax.dynamic_slice_in_dim(lengths, start, span, 0)[None, :]
        amp_right = lax.dynamic_slice_in_dim(amplitude, start, span, 0)[None, :]
        denom = left * left + right * right
        vals = (
            amplitude[:, None]
            * amp_right
            * jnp.sqrt(2.0 * left * right / denom)
            * jnp.exp(-diff * diff / denom)
        )
        return vals.astype(BF16)

    return lax.map(one_block, jnp.arange(count, dtype=jnp.int32))


def data_rows(packed, resp_perm, stud_perm, blocks, order, inverse):
    rows, chans = packed.shape
    nblk, width = (blocks.shape[0], blocks.shape[1])
    moved = jnp.take(packed, order, axis=1).reshape(rows, nblk, width)
    product = jnp.einsum("rbi,bij->rbj", moved, blocks, preferred_element_type=F32).reshape(rows, chans)
    permuted = stud_perm.astype(F32) * (product - resp_perm.astype(F32))
    return jnp.take(permuted, inverse, axis=1).astype(BF16)


def general(gains, response, student, blocks, order, lower, upper, lengths, amplitude):
    nwide = lax.axis_size("wide")
    chd, epochs = gains.shape
    epd = epochs // nwide
    chans = chd * nwide
    inverse = jnp.zeros((chans,), jnp.int32).at[order].set(jnp.arange(chans, dtype=jnp.int32))
    resp_perm = jnp.take(response, order, axis=1)
    stud_perm = jnp.take(student, order, axis=1)
    span = min(256, epochs)
    kernel_stack = covar_stack(lengths, amplitude, span)
    current = gains
    for step in range(ITERS):
        packed = current.astype(BF16).reshape(chd, nwide, epd)
        got = (
            lax.all_to_all(packed, "wide", split_axis=1, concat_axis=0, tiled=True)
            .reshape(chans, epd)
            .T
        )
        misfit_rows = data_rows(got, resp_perm, stud_perm, blocks, order, inverse)
        misfit = lax.all_to_all(
            misfit_rows.T.reshape(chans, 1, epd), "wide", split_axis=0, concat_axis=1, tiled=True
        ).reshape(chd, epochs)
        smoothed = jnp.einsum("ce,bes->cbs", misfit, kernel_stack, preferred_element_type=F32).reshape(
            chd, epochs
        )
        current = jnp.clip(current - 0.02 * smoothed, lower[:, None], upper[:, None])
    return current


def per_device(*args):
    ndev = lax.axis_size("wide")
    chd, epochs = args[0].shape
    fits = ndev >= 4 and ndev & (ndev - 1) == 0 and chd % 128 == 0 and (epochs // ndev) % 256 == 0
    return (fast if fits else general)(*args)


def solution(mesh):
    placed = (
        P(("half", "wide"), None),
        P("wide", "half"),
        P("wide", "half"),
        P("half", None, None),
        P("half"),
        P(("half", "wide")),
        P(("half", "wide")),
        P(),
        P(),
    )
    return jax.shard_map(
        per_device, mesh=mesh, in_specs=placed, out_specs=P(("half", "wide"), None), check_vma=False
    )
```

```python
import math
import jax
import jax.numpy as jnp
from jax import lax
from jax.experimental import pallas as pl
from jax.experimental.pallas import tpu as pltpu
from jax.sharding import PartitionSpec as P

ITERS = 2
LN2 = math.log(2.0)
F32 = jnp.float32
BF16 = jnp.bfloat16


def params(mib=8):
    return pltpu.CompilerParams(vmem_limit_bytes=mib * 1024 * 1024)


CHEAP = pl.CostEstimate(flops=1, bytes_accessed=1, transcendentals=0)
SMEM = pl.BlockSpec(memory_space=pltpu.SMEM)
VMEM = pl.BlockSpec(memory_space=pltpu.VMEM)
HBM = pl.BlockSpec(memory_space=pltpu.HBM)


def dot(a, b):
    return jnp.dot(a, b, preferred_element_type=F32)


def column(row):
    n = row.shape[1]
    return jnp.broadcast_to(row, (n, n)).T[:, :1]


def pack(me, gains, ndev, epd):
    chd, total = gains.shape
    half = ndev // 2
    order = [*range(1, ndev), 0]

    def body(me_ref, gains_ref, *refs):
        outs, kept, sems = refs[:ndev], refs[ndev : ndev + 2], refs[ndev + 2]

        def place(r):
            return kept[r // half].at[:, pl.ds(r % half * epd, epd)]

        def copy(r):
            theirs = pl.ds(pl.multiple_of((me_ref[0] ^ r) * epd, epd), epd)
            return pltpu.make_async_copy(gains_ref.at[:, theirs], place(r), sems.at[r])

        for r in order:
            copy(r).start()
        for r in order:
            copy(r).wait()
            outs[r][...] = place(r)[...].astype(BF16)

    return pl.pallas_call(
        body,
        out_shape=[jax.ShapeDtypeStruct((chd, epd), BF16)] * ndev + [pltpu.VMEM((chd, total // 2), F32)] * 2,
        in_specs=[SMEM, HBM],
        out_specs=[VMEM] * (ndev + 2),
        scratch_shapes=[pltpu.SemaphoreType.DMA((ndev,))],
        compiler_params=params(),
        cost_estimate=CHEAP,
        name="pack_gains",
    )(me, pltpu.with_memory_space_constraint(gains, pltpu.HBM))


def flip(me, data, ndev, factors=None):
    epd, chans = data.shape
    chd = chans // ndev
    kind = BF16 if factors is None else F32
    more = [] if factors is None else [factors]

    def body(me_ref, data_ref, *refs):
        for r in range(ndev):
            cols = pl.ds(pl.multiple_of((me_ref[0] ^ r) * chd, chd), chd)
            out = data_ref[:, cols].astype(F32).T
            if more:
                out = out * refs[0][:, pl.ds(pl.multiple_of(me_ref[0] * epd, epd), epd)]
            refs[-1][pl.ds(r * chd, chd), :] = out.astype(kind)

    return pl.pallas_call(
        body,
        out_shape=pltpu.VMEM((chans, epd), kind),
        in_specs=[SMEM, VMEM] + [VMEM] * len(more),
        out_specs=VMEM,
        compiler_params=params(),
        cost_estimate=CHEAP,
        name="flip",
    )(me, data, *more)


def dense(me, blocks, channels, ndev):
    nblk, width, _ = blocks.shape
    chans = nblk * width
    chd = chans // ndev

    def body(me_ref, blocks_ref, order_ref, out_ref, left_ref, hot_ref):
        def names_along(dim, shape):
            at = lax.broadcasted_iota(jnp.int32, shape, dim)
            return (((at // chd) ^ me_ref[0]) * chd + at % chd).astype(F32)

        down = names_along(0, (chans, width))
        along = names_along(1, (width, chans))
        for b in range(nblk):
            span = pl.ds(b * width, width)
            names = order_ref[:, span].astype(F32)
            hot = jnp.where(down == names, 1.0, 0.0).astype(BF16)
            left_ref[:, span] = dot(hot, blocks_ref[b]).astype(BF16)
            hot_ref[span, :] = jnp.where(along == column(names), 1.0, 0.0).astype(BF16)
        for r in range(0, ndev, 2):
            rows = pl.ds(r * chd, 2 * chd)
            out_ref[rows, :] = dot(left_ref[rows, :], hot_ref[...]).astype(BF16)

    return pl.pallas_call(
        body,
        out_shape=pltpu.VMEM((chans, chans), BF16),
        in_specs=[SMEM, VMEM, VMEM],
        out_specs=VMEM,
        scratch_shapes=[pltpu.VMEM((chans, chans), BF16)] * 2,
        compiler_params=params(),
        cost_estimate=CHEAP,
        name="dense_blocks",
    )(me, blocks, channels[None, :])


def distances(total):
    def body(out_ref):
        for c in range(0, 2 * total, 128):
            row = lax.broadcasted_iota(jnp.int32, (128, 128), 0)
            away = (row - lax.broadcasted_iota(jnp.int32, (128, 128), 1) + (total - c)).astype(F32)
            out_ref[:, pl.ds(c, 128)] = -away * away

    return pl.pallas_call(
        body,
        out_shape=pltpu.VMEM((128, 2 * total), F32),
        out_specs=VMEM,
        compiler_params=params(),
        cost_estimate=CHEAP,
        name="distances",
    )()


def covar_tiles(me_ref, away_ref, squares_ref, own_ref, offset, k, others, epd, store):
    group = 32
    total = squares_ref.shape[1]
    base = (me_ref[0] ^ offset) * epd + k * 128
    span = pl.ds(pl.multiple_of(base, 128), 128)
    own_ref[...] = jnp.broadcast_to(squares_ref[:, span], (128, 128)).T
    for r in others:
        first = (me_ref[0] ^ r) * epd
        for c in range(0, epd, 128):
            theirs = squares_ref[:, pl.ds(pl.multiple_of(first + c, 128), 128)]
            window = pl.ds(pl.multiple_of(total + first + c - base, 128), 128)
            parts = []
            for g in range(0, 128, group):
                rows = pl.ds(g, group)
                q = lax.rsqrt(own_ref[rows, :] + theirs)
                parts.append((q * jnp.exp2(away_ref[rows, window] * (q * q))).astype(BF16))
            store(r, c, jnp.concatenate(parts, axis=0))


def covar_own(me, away, squares, offsets, epd):
    per = epd // 128
    first = offsets[0]
    count = len(offsets) * epd

    def body(me_ref, away_ref, squares_ref, out_ref, own_ref):
        for n, offset in enumerate(offsets):

            def block(k, _):
                mine = pl.ds(pl.multiple_of(n * epd + k * 128, 128), 128)

                def store(r, c, tile):
                    theirs = pl.ds((r - first) * epd + c, 128)
                    out_ref[mine, theirs] = tile
                    if r != offset:
                        out_ref[theirs, mine] = tile.T

                covar_tiles(me_ref, away_ref, squares_ref, own_ref, offset, k, offsets[n:], epd, store)
                return 0

            lax.fori_loop(0, per, block, 0)

    return pl.pallas_call(
        body,
        out_shape=pltpu.VMEM((count, count), BF16),
        in_specs=[SMEM, VMEM, VMEM],
        out_specs=VMEM,
        scratch_shapes=[pltpu.VMEM((128, 128), F32)],
        compiler_params=params(),
        cost_estimate=CHEAP,
        name="covar_own",
    )(me, away, squares)


def covar_cross(me, away, squares, near, far, epd):
    per = epd // 128
    shape = (len(near) * epd, len(far) * epd)

    def body(me_ref, away_ref, squares_ref, out_ref, flip_ref, own_ref):
        def block(n, _):
            mine = pl.ds(pl.multiple_of(n * 128, 128), 128)

            def store(r, c, tile):
                theirs = pl.ds((r - far[0]) * epd + c, 128)
                out_ref[mine, theirs] = tile
                flip_ref[theirs, mine] = tile.T

            covar_tiles(me_ref, away_ref, squares_ref, own_ref, near[0] + n // per, n % per, far, epd, store)
            return 0

        lax.fori_loop(0, shape[0] // 128, block, 0)

    return pl.pallas_call(
        body,
        out_shape=[pltpu.VMEM(shape, BF16), pltpu.VMEM(shape[::-1], BF16)],
        in_specs=[SMEM, VMEM, VMEM],
        out_specs=[VMEM] * 2,
        scratch_shapes=[pltpu.VMEM((128, 128), F32)],
        compiler_params=params(),
        cost_estimate=CHEAP,
        name="covar_cross",
    )(me, away, squares)


def normal(weights, pieces, resp, stud, order):
    ndev = len(pieces)
    chd, epd = pieces[0].shape
    chans = ndev * chd

    def body(*refs):
        ins, (w_ref, resp_ref, stud_ref), outs, got = refs[:ndev], refs[ndev : ndev + 3], refs[ndev + 3 : -1], refs[-1]
        for r, ref in zip([*order, 0], ins):
            got[pl.ds(r * chd, chd), :] = ref[...]
        for r in range(ndev):
            rows = pl.ds(r * chd, chd)
            product = dot(w_ref[rows, :], got[...])
            outs[r][...] = (stud_ref[rows, :] * (product - resp_ref[rows, :].astype(F32))).astype(BF16)

    return list(
        pl.pallas_call(
            body,
            out_shape=[jax.ShapeDtypeStruct((chd, epd), BF16)] * ndev,
            in_specs=[VMEM] * (3 + ndev),
            out_specs=[VMEM] * ndev,
            scratch_shapes=[pltpu.VMEM((chans, epd), BF16)],
            compiler_params=params(),
            cost_estimate=CHEAP,
            name="normal_step",
        )(*[pieces[r] for r in [*order, 0]], weights, resp, stud)
    )


def terms_of(offsets, half):
    runs = []
    for r in sorted(offsets):
        if runs and runs[-1][1][-1] == r - 1 and r != half:
            runs[-1][1].append(r)
        else:
            runs.append((r // half, [r], r % half))
    return runs


def products(got, offsets, rows, refs):
    half = len(got) // 2
    epd = got[0].shape[1]
    pieces = {r: next(refs) for r in offsets}
    sides = [[next(refs) for _ in side] for side in rows]
    return [
        (
            jnp.concatenate([pieces[r][...] for r in run], axis=1),
            sides[side],
            pl.ds(at * epd, len(run) * epd),
        )
        for side, run, at in terms_of(offsets, half)
    ]


def partial(got, offsets, rows, before):
    chd, epd = got[0].shape
    span = max(block.shape[1] for side in rows for block in side)
    blocks = max(len(side) for side in rows)
    args = [got[r] for r in offsets] + [block for side in rows for block in side]
    more = [] if before is None else [before]

    def body(*refs):
        given = iter(refs)
        terms = products(got, offsets, rows, given)
        before_ref, out_ref = [next(given) for _ in more], refs[-1]
        for b in range(blocks):
            for c in range(0, span, epd):
                cols = pl.ds(b * span + c, epd)
                acc = before_ref[0][:, cols] if more else None
                for left, side, at in terms:
                    term = dot(left, side[b][at, pl.ds(c, epd)])
                    acc = term if acc is None else acc + term
                out_ref[:, cols] = acc

    return pl.pallas_call(
        body,
        out_shape=pltpu.VMEM((chd, blocks * span), F32),
        in_specs=[VMEM] * (len(args) + len(more)),
        out_specs=VMEM,
        compiler_params=params(),
        cost_estimate=CHEAP,
        name="smooth_part",
    )(*args, *more)


def update(me, got, offsets, rows, before, current, factors, lower, upper, last):
    chd, epd = got[0].shape
    ndev = len(got)
    total = ndev * epd
    wide = current[0].shape[1]
    span = max(block.shape[1] for side in rows for block in side)
    args = [got[r] for r in offsets] + [block for side in rows for block in side]

    def body(me_ref, *refs):
        given = iter(refs)
        terms = products(got, offsets, rows, given)
        before_ref = next(given)
        cur_refs = [next(given) for _ in current]
        factors_ref, low, high = next(given), column(next(given)[...]), column(next(given)[...])
        outs = list(given)
        copies = []
        for n in range(ndev):
            cols = pl.ds(n * epd, epd)
            block, c = divmod(n * epd, span)
            acc = before_ref[:, cols]
            for left, side, at in terms:
                acc = acc + dot(left, side[block][at, pl.ds(c, epd)])
            theirs = pl.ds(pl.multiple_of((me_ref[0] ^ n) * epd, epd), epd)
            gone = acc * (0.02 * factors_ref[:, theirs])
            new = jnp.clip(cur_refs[n * epd // wide][:, pl.ds(n * epd % wide, epd)] - gone, low, high)
            if last:
                out_ref, stage, sems = outs
                stage[:, cols] = new
                copies.append(pltpu.make_async_copy(stage.at[:, cols], out_ref.at[:, theirs], sems.at[n]))
                copies[-1].start()
            else:
                outs[0][:, cols] = new
                outs[1 + n][...] = new.astype(BF16)
        for copy in copies:
            copy.wait()

    if last:
        shapes, specs = [jax.ShapeDtypeStruct((chd, total), F32)], [HBM]
        scratch = [pltpu.VMEM((chd, total), F32), pltpu.SemaphoreType.DMA((ndev,))]
    else:
        shapes = [pltpu.VMEM((chd, total), F32)] + [jax.ShapeDtypeStruct((chd, epd), BF16)] * ndev
        specs, scratch = [VMEM] * (1 + ndev), []
    out, *pieces = pl.pallas_call(
        body,
        out_shape=shapes,
        in_specs=[SMEM] + [VMEM] * (len(args) + len(current) + 4),
        out_specs=specs,
        scratch_shapes=scratch,
        compiler_params=params(),
        cost_estimate=CHEAP,
        name="update",
    )(me, *args, before, *current, factors, lower, upper)
    return out, pieces


def swap(pieces):
    ndev = len(pieces)
    return [pieces[0]] + [
        lax.ppermute(pieces[r], "wide", [(i, i ^ r) for i in range(ndev)]) for r in range(1, ndev)
    ]


CFG = {'o1': '6712345', 'g2': '67,0123,4,5', 't2': (4,), 'n2': 1, 'o3': '6712345', 'g4': '67,0123,4,5'}


def fast(gains, response, student, blocks, channels, lower, upper, lengths, amplitude):
    ndev = lax.axis_size("wide")
    epd = gains.shape[1] // ndev
    half = ndev // 2
    near, far = list(range(half)), list(range(half, ndev))
    me = lax.axis_index("wide").astype(jnp.int32).reshape(1)
    low, high = lower[None, :], upper[None, :]
    squares = (lengths * lengths * LN2)[None, :]
    factors = (amplitude * jnp.sqrt(lengths * math.sqrt(2.0 * LN2)))[None, :]
    tied = lax.optimization_barrier
    digits = lambda text: [int(c) for c in text]
    order = digits(CFG["o1"])
    groups2 = [digits(g) for g in CFG["g2"].split(",")]
    groups4 = [digits(g) for g in CFG["g4"].split(",")]

    *packed, kept_near, kept_far = pack(me, gains, ndev, epd)
    got = swap(packed)
    weights = dense(me, blocks, channels, ndev)
    resp = flip(me, response, ndev)
    stud = flip(me, student, ndev, factors)
    away = distances(gains.shape[1])
    near_far, far_near = covar_cross(me, away, squares, near, far, epd)
    arrived, near_far, far_near = tied(([got[r] for r in order], near_far, far_near))
    got = {0: got[0], **dict(zip(order, arrived))}

    misfit = normal(weights, got, resp, stud, order)
    part, misfit = tied((squares, misfit))
    far_far = covar_own(me, away, part, far, epd)
    for r in CFG["t2"]:
        misfit[r], far_far = tied((misfit[r], far_far))
    n2 = CFG["n2"]
    if n2 == 0:
        part, far_far = tied((squares, far_far))
        near_near = covar_own(me, away, part, near, epd)
    if n2 == -1:
        near_near = covar_own(me, away, squares, near, epd)
        misfit[0], near_near = tied((misfit[0], near_near))
    got = swap(misfit)
    far_rows = [far_near, far_far]
    total = None
    for n, group in enumerate(groups2[:-1]):
        if n == n2 and n2 > 0:
            part, total = tied((squares, total))
            near_near = covar_own(me, away, part, near, epd)
        rows = [[], far_rows] if min(group) >= half else [[near_near, near_far], far_rows]
        total = partial(got, group, rows, total)
    rows = [[near_near, near_far], far_rows]
    kept, packed = update(me, got, groups2[-1], rows, total, [kept_near, kept_far], factors, low, high, False)

    order = digits(CFG["o3"])
    got = swap(normal(weights, swap(packed), resp, stud, order))
    total = None
    for group in groups4[:-1]:
        total = partial(got, group, rows, total)
    out, _ = update(me, got, groups4[-1], rows, total, [kept], factors, low, high, True)
    return out


def covar_stack(lengths, amplitude, span):
    total = lengths.shape[0]
    count = total // span
    rows = jnp.arange(total, dtype=jnp.int32)

    def one_block(index):
        start = index * span
        cols = start + jnp.arange(span, dtype=jnp.int32)
        diff = (rows[:, None] - cols[None, :]).astype(lengths.dtype)
        left = lengths[:, None]
        right = lax.dynamic_slice_in_dim(lengths, start, span, 0)[None, :]
        amp_right = lax.dynamic_slice_in_dim(amplitude, start, span, 0)[None, :]
        denom = left * left + right * right
        vals = (
            amplitude[:, None]
            * amp_right
            * jnp.sqrt(2.0 * left * right / denom)
            * jnp.exp(-diff * diff / denom)
        )
        return vals.astype(BF16)

    return lax.map(one_block, jnp.arange(count, dtype=jnp.int32))


def data_rows(packed, resp_perm, stud_perm, blocks, order, inverse):
    rows, chans = packed.shape
    nblk, width = (blocks.shape[0], blocks.shape[1])
    moved = jnp.take(packed, order, axis=1).reshape(rows, nblk, width)
    product = jnp.einsum("rbi,bij->rbj", moved, blocks, preferred_element_type=F32).reshape(rows, chans)
    permuted = stud_perm.astype(F32) * (product - resp_perm.astype(F32))
    return jnp.take(permuted, inverse, axis=1).astype(BF16)


def general(gains, response, student, blocks, order, lower, upper, lengths, amplitude):
    nwide = lax.axis_size("wide")
    chd, epochs = gains.shape
    epd = epochs // nwide
    chans = chd * nwide
    inverse = jnp.zeros((chans,), jnp.int32).at[order].set(jnp.arange(chans, dtype=jnp.int32))
    resp_perm = jnp.take(response, order, axis=1)
    stud_perm = jnp.take(student, order, axis=1)
    span = min(256, epochs)
    kernel_stack = covar_stack(lengths, amplitude, span)
    current = gains
    for step in range(ITERS):
        packed = current.astype(BF16).reshape(chd, nwide, epd)
        got = (
            lax.all_to_all(packed, "wide", split_axis=1, concat_axis=0, tiled=True)
            .reshape(chans, epd)
            .T
        )
        misfit_rows = data_rows(got, resp_perm, stud_perm, blocks, order, inverse)
        misfit = lax.all_to_all(
            misfit_rows.T.reshape(chans, 1, epd), "wide", split_axis=0, concat_axis=1, tiled=True
        ).reshape(chd, epochs)
        smoothed = jnp.einsum("ce,bes->cbs", misfit, kernel_stack, preferred_element_type=F32).reshape(
            chd, epochs
        )
        current = jnp.clip(current - 0.02 * smoothed, lower[:, None], upper[:, None])
    return current


def per_device(*args):
    ndev = lax.axis_size("wide")
    chd, epochs = args[0].shape
    fits = ndev >= 8 and ndev & (ndev - 1) == 0 and chd % 128 == 0 and (epochs // ndev) % 256 == 0
    return (fast if fits else general)(*args)


def solution(mesh):
    placed = (
        P(("half", "wide"), None),
        P("wide", "half"),
        P("wide", "half"),
        P("half", None, None),
        P("half"),
        P(("half", "wide")),
        P(("half", "wide")),
        P(),
        P(),
    )
    return jax.shard_map(
        per_device, mesh=mesh, in_specs=placed, out_specs=P(("half", "wide"), None), check_vma=False
    )
```

```python
import math
import jax
import jax.numpy as jnp
from jax import lax
from jax.experimental import pallas as pl
from jax.experimental.pallas import tpu as pltpu
from jax.sharding import PartitionSpec as P

ITERS = 2
LN2 = math.log(2.0)
F32 = jnp.float32
BF16 = jnp.bfloat16


def params(mib=8):
    return pltpu.CompilerParams(vmem_limit_bytes=mib * 1024 * 1024)


CHEAP = pl.CostEstimate(flops=1, bytes_accessed=1, transcendentals=0)
SMEM = pl.BlockSpec(memory_space=pltpu.SMEM)
VMEM = pl.BlockSpec(memory_space=pltpu.VMEM)
HBM = pl.BlockSpec(memory_space=pltpu.HBM)


def dot(a, b):
    return jnp.dot(a, b, preferred_element_type=F32)


def column(row):
    n = row.shape[1]
    return jnp.broadcast_to(row, (n, n)).T[:, :1]


def pack(me, gains, ndev, epd):
    chd, total = gains.shape
    half = ndev // 2
    order = [*range(1, ndev), 0]

    def body(me_ref, gains_ref, *refs):
        outs, kept, sems = refs[:ndev], refs[ndev : ndev + 2], refs[ndev + 2]

        def place(r):
            return kept[r // half].at[:, pl.ds(r % half * epd, epd)]

        def copy(r):
            theirs = pl.ds(pl.multiple_of((me_ref[0] ^ r) * epd, epd), epd)
            return pltpu.make_async_copy(gains_ref.at[:, theirs], place(r), sems.at[r])

        for r in order:
            copy(r).start()
        for r in order:
            copy(r).wait()
            outs[r][...] = place(r)[...].astype(BF16)

    return pl.pallas_call(
        body,
        out_shape=[jax.ShapeDtypeStruct((chd, epd), BF16)] * ndev + [pltpu.VMEM((chd, total // 2), F32)] * 2,
        in_specs=[SMEM, HBM],
        out_specs=[VMEM] * (ndev + 2),
        scratch_shapes=[pltpu.SemaphoreType.DMA((ndev,))],
        compiler_params=params(),
        cost_estimate=CHEAP,
        name="pack_gains",
    )(me, pltpu.with_memory_space_constraint(gains, pltpu.HBM))


def flip(me, data, ndev, factors=None):
    epd, chans = data.shape
    chd = chans // ndev
    kind = BF16 if factors is None else F32
    more = [] if factors is None else [factors]

    def body(me_ref, data_ref, *refs):
        for r in range(ndev):
            cols = pl.ds(pl.multiple_of((me_ref[0] ^ r) * chd, chd), chd)
            out = data_ref[:, cols].astype(F32).T
            if more:
                out = out * refs[0][:, pl.ds(pl.multiple_of(me_ref[0] * epd, epd), epd)]
            refs[-1][pl.ds(r * chd, chd), :] = out.astype(kind)

    return pl.pallas_call(
        body,
        out_shape=pltpu.VMEM((chans, epd), kind),
        in_specs=[SMEM, VMEM] + [VMEM] * len(more),
        out_specs=VMEM,
        compiler_params=params(),
        cost_estimate=CHEAP,
        name="flip",
    )(me, data, *more)


def dense(me, blocks, channels, ndev):
    nblk, width, _ = blocks.shape
    chans = nblk * width
    chd = chans // ndev

    def body(me_ref, blocks_ref, order_ref, out_ref, left_ref, hot_ref):
        def names_along(dim, shape):
            at = lax.broadcasted_iota(jnp.int32, shape, dim)
            return (((at // chd) ^ me_ref[0]) * chd + at % chd).astype(F32)

        down = names_along(0, (chans, width))
        along = names_along(1, (width, chans))
        for b in range(nblk):
            span = pl.ds(b * width, width)
            names = order_ref[:, span].astype(F32)
            hot = jnp.where(down == names, 1.0, 0.0).astype(BF16)
            left_ref[:, span] = dot(hot, blocks_ref[b]).astype(BF16)
            hot_ref[span, :] = jnp.where(along == column(names), 1.0, 0.0).astype(BF16)
        for r in range(0, ndev, 2):
            rows = pl.ds(r * chd, 2 * chd)
            out_ref[rows, :] = dot(left_ref[rows, :], hot_ref[...]).astype(BF16)

    return pl.pallas_call(
        body,
        out_shape=pltpu.VMEM((chans, chans), BF16),
        in_specs=[SMEM, VMEM, VMEM],
        out_specs=VMEM,
        scratch_shapes=[pltpu.VMEM((chans, chans), BF16)] * 2,
        compiler_params=params(),
        cost_estimate=CHEAP,
        name="dense_blocks",
    )(me, blocks, channels[None, :])


def distances(total):
    def body(out_ref):
        for c in range(0, 2 * total, 128):
            row = lax.broadcasted_iota(jnp.int32, (128, 128), 0)
            away = (row - lax.broadcasted_iota(jnp.int32, (128, 128), 1) + (total - c)).astype(F32)
            out_ref[:, pl.ds(c, 128)] = -away * away

    return pl.pallas_call(
        body,
        out_shape=pltpu.VMEM((128, 2 * total), F32),
        out_specs=VMEM,
        compiler_params=params(),
        cost_estimate=CHEAP,
        name="distances",
    )()


def covar_tiles(me_ref, away_ref, squares_ref, own_ref, offset, k, others, epd, store):
    group = 32
    total = squares_ref.shape[1]
    base = (me_ref[0] ^ offset) * epd + k * 128
    span = pl.ds(pl.multiple_of(base, 128), 128)
    own_ref[...] = jnp.broadcast_to(squares_ref[:, span], (128, 128)).T
    for r in others:
        first = (me_ref[0] ^ r) * epd
        for c in range(0, epd, 128):
            theirs = squares_ref[:, pl.ds(pl.multiple_of(first + c, 128), 128)]
            window = pl.ds(pl.multiple_of(total + first + c - base, 128), 128)
            parts = []
            for g in range(0, 128, group):
                rows = pl.ds(g, group)
                q = lax.rsqrt(own_ref[rows, :] + theirs)
                parts.append((q * jnp.exp2(away_ref[rows, window] * (q * q))).astype(BF16))
            store(r, c, jnp.concatenate(parts, axis=0))


def covar_own(me, away, squares, offsets, epd):
    per = epd // 128
    first = offsets[0]
    count = len(offsets) * epd

    def body(me_ref, away_ref, squares_ref, out_ref, own_ref):
        for n, offset in enumerate(offsets):

            def block(k, _):
                mine = pl.ds(pl.multiple_of(n * epd + k * 128, 128), 128)

                def store(r, c, tile):
                    theirs = pl.ds((r - first) * epd + c, 128)
                    out_ref[mine, theirs] = tile
                    if r != offset:
                        out_ref[theirs, mine] = tile.T

                covar_tiles(me_ref, away_ref, squares_ref, own_ref, offset, k, offsets[n:], epd, store)
                return 0

            lax.fori_loop(0, per, block, 0)

    return pl.pallas_call(
        body,
        out_shape=pltpu.VMEM((count, count), BF16),
        in_specs=[SMEM, VMEM, VMEM],
        out_specs=VMEM,
        scratch_shapes=[pltpu.VMEM((128, 128), F32)],
        compiler_params=params(),
        cost_estimate=CHEAP,
        name="covar_own",
    )(me, away, squares)


def covar_cross(me, away, squares, near, far, epd):
    per = epd // 128
    shape = (len(near) * epd, len(far) * epd)

    def body(me_ref, away_ref, squares_ref, out_ref, flip_ref, own_ref):
        def block(n, _):
            mine = pl.ds(pl.multiple_of(n * 128, 128), 128)

            def store(r, c, tile):
                theirs = pl.ds((r - far[0]) * epd + c, 128)
                out_ref[mine, theirs] = tile
                flip_ref[theirs, mine] = tile.T

            covar_tiles(me_ref, away_ref, squares_ref, own_ref, near[0] + n // per, n % per, far, epd, store)
            return 0

        lax.fori_loop(0, shape[0] // 128, block, 0)

    return pl.pallas_call(
        body,
        out_shape=[pltpu.VMEM(shape, BF16), pltpu.VMEM(shape[::-1], BF16)],
        in_specs=[SMEM, VMEM, VMEM],
        out_specs=[VMEM] * 2,
        scratch_shapes=[pltpu.VMEM((128, 128), F32)],
        compiler_params=params(),
        cost_estimate=CHEAP,
        name="covar_cross",
    )(me, away, squares)


def normal(weights, pieces, resp, stud, order):
    ndev = len(pieces)
    chd, epd = pieces[0].shape
    chans = ndev * chd

    def body(*refs):
        ins, (w_ref, resp_ref, stud_ref), outs, got = refs[:ndev], refs[ndev : ndev + 3], refs[ndev + 3 : -1], refs[-1]
        for r, ref in zip([*order, 0], ins):
            got[pl.ds(r * chd, chd), :] = ref[...]
        for r in range(ndev):
            rows = pl.ds(r * chd, chd)
            product = dot(w_ref[rows, :], got[...])
            outs[r][...] = (stud_ref[rows, :] * (product - resp_ref[rows, :].astype(F32))).astype(BF16)

    return list(
        pl.pallas_call(
            body,
            out_shape=[jax.ShapeDtypeStruct((chd, epd), BF16)] * ndev,
            in_specs=[VMEM] * (3 + ndev),
            out_specs=[VMEM] * ndev,
            scratch_shapes=[pltpu.VMEM((chans, epd), BF16)],
            compiler_params=params(),
            cost_estimate=CHEAP,
            name="normal_step",
        )(*[pieces[r] for r in [*order, 0]], weights, resp, stud)
    )


def terms_of(offsets, half):
    runs = []
    for r in sorted(offsets):
        if runs and runs[-1][1][-1] == r - 1 and r != half:
            runs[-1][1].append(r)
        else:
            runs.append((r // half, [r], r % half))
    return runs


def sides_of(offsets, half):
    return sorted({r // half for r in offsets})


def products(got, offsets, rows, refs):
    half = len(got) // 2
    epd = got[0].shape[1]
    pieces = {r: next(refs) for r in offsets}
    sides = {side: [next(refs) for _ in rows[side]] for side in sides_of(offsets, half)}
    return [
        (
            jnp.concatenate([pieces[r][...] for r in run], axis=1),
            sides[side],
            pl.ds(at * epd, len(run) * epd),
        )
        for side, run, at in terms_of(offsets, half)
    ]


def partial(got, offsets, rows, before):
    chd, epd = got[0].shape
    span = max(block.shape[1] for side in rows for block in side)
    blocks = max(len(side) for side in rows)
    args = [got[r] for r in offsets] + [block for side in sides_of(offsets, len(got) // 2) for block in rows[side]]
    more = [] if before is None else [before]

    def body(*refs):
        given = iter(refs)
        terms = products(got, offsets, rows, given)
        before_ref, out_ref = [next(given) for _ in more], refs[-1]
        for b in range(blocks):
            for c in range(0, span, epd):
                cols = pl.ds(b * span + c, epd)
                acc = before_ref[0][:, cols] if more else None
                for left, side, at in terms:
                    term = dot(left, side[b][at, pl.ds(c, epd)])
                    acc = term if acc is None else acc + term
                out_ref[:, cols] = acc

    return pl.pallas_call(
        body,
        out_shape=pltpu.VMEM((chd, blocks * span), F32),
        in_specs=[VMEM] * (len(args) + len(more)),
        out_specs=VMEM,
        compiler_params=params(),
        cost_estimate=CHEAP,
        name="smooth_part",
    )(*args, *more)


def update(me, got, offsets, rows, before, current, factors, lower, upper, last):
    chd, epd = got[0].shape
    ndev = len(got)
    total = ndev * epd
    wide = current[0].shape[1]
    span = max(block.shape[1] for side in rows for block in side)
    args = [got[r] for r in offsets] + [block for side in sides_of(offsets, len(got) // 2) for block in rows[side]]

    def body(me_ref, *refs):
        given = iter(refs)
        terms = products(got, offsets, rows, given)
        before_ref = next(given)
        cur_refs = [next(given) for _ in current]
        factors_ref, low, high = next(given), column(next(given)[...]), column(next(given)[...])
        outs = list(given)
        copies = []
        for n in range(ndev):
            cols = pl.ds(n * epd, epd)
            block, c = divmod(n * epd, span)
            acc = before_ref[:, cols]
            for left, side, at in terms:
                acc = acc + dot(left, side[block][at, pl.ds(c, epd)])
            theirs = pl.ds(pl.multiple_of((me_ref[0] ^ n) * epd, epd), epd)
            gone = acc * (0.02 * factors_ref[:, theirs])
            new = jnp.clip(cur_refs[n * epd // wide][:, pl.ds(n * epd % wide, epd)] - gone, low, high)
            if last:
                out_ref, stage, sems = outs
                stage[:, cols] = new
                copies.append(pltpu.make_async_copy(stage.at[:, cols], out_ref.at[:, theirs], sems.at[n]))
                copies[-1].start()
            else:
                outs[0][:, cols] = new
                outs[1 + n][...] = new.astype(BF16)
        for copy in copies:
            copy.wait()

    if last:
        shapes, specs = [jax.ShapeDtypeStruct((chd, total), F32)], [HBM]
        scratch = [pltpu.VMEM((chd, total), F32), pltpu.SemaphoreType.DMA((ndev,))]
    else:
        shapes = [pltpu.VMEM((chd, total), F32)] + [jax.ShapeDtypeStruct((chd, epd), BF16)] * ndev
        specs, scratch = [VMEM] * (1 + ndev), []
    out, *pieces = pl.pallas_call(
        body,
        out_shape=shapes,
        in_specs=[SMEM] + [VMEM] * (len(args) + len(current) + 4),
        out_specs=specs,
        scratch_shapes=scratch,
        compiler_params=params(),
        cost_estimate=CHEAP,
        name="update",
    )(me, *args, before, *current, factors, lower, upper)
    return out, pieces


def swap(pieces):
    ndev = len(pieces)
    return [pieces[0]] + [
        lax.ppermute(pieces[r], "wide", [(i, i ^ r) for i in range(ndev)]) for r in range(1, ndev)
    ]


def fast(gains, response, student, blocks, channels, lower, upper, lengths, amplitude):
    ndev = lax.axis_size("wide")
    epd = gains.shape[1] // ndev
    half = ndev // 2
    near, far = list(range(half)), list(range(half, ndev))
    me = lax.axis_index("wide").astype(jnp.int32).reshape(1)
    low, high = lower[None, :], upper[None, :]
    squares = (lengths * lengths * LN2)[None, :]
    factors = (amplitude * jnp.sqrt(lengths * math.sqrt(2.0 * LN2)))[None, :]
    tied = lax.optimization_barrier

    order = [*far[half // 2 :], *near[1:], *far[: half // 2]]
    groups = [far[:1], near, far[1:-1]]
    latest = far[-1:]

    *packed, kept_near, kept_far = pack(me, gains, ndev, epd)
    got = swap(packed)
    weights = dense(me, blocks, channels, ndev)
    resp = flip(me, response, ndev)
    stud = flip(me, student, ndev, factors)
    away = distances(gains.shape[1])
    near_far, far_near = covar_cross(me, away, squares, near, far, epd)
    arrived, near_far, far_near = tied(([got[r] for r in order], near_far, far_near))
    got = {0: got[0], **dict(zip(order, arrived))}

    misfit = normal(weights, got, resp, stud, order)
    part, misfit = tied((squares, misfit))
    far_far = covar_own(me, away, part, far, epd)
    misfit[-1], far_far = tied((misfit[-1], far_far))
    near_near = covar_own(me, away, squares, near, epd)
    misfit[0], near_near = tied((misfit[0], near_near))
    got = swap(misfit)
    rows = [[near_near, near_far], [far_near, far_far]]
    total = None
    for group in groups:
        total = partial(got, group, rows, total)
    current = [kept_near, kept_far]
    current, packed = update(me, got, latest, rows, total, current, factors, low, high, False)

    order = [*far[:0:-1], *near[1:], far[0]]
    got = swap(normal(weights, swap(packed), resp, stud, order))
    total = None
    for group in groups:
        total = partial(got, group, rows, total)
    out, _ = update(me, got, latest, rows, total, [current], factors, low, high, True)
    return out


def covar_stack(lengths, amplitude, span):
    total = lengths.shape[0]
    count = total // span
    rows = jnp.arange(total, dtype=jnp.int32)

    def one_block(index):
        start = index * span
        cols = start + jnp.arange(span, dtype=jnp.int32)
        diff = (rows[:, None] - cols[None, :]).astype(lengths.dtype)
        left = lengths[:, None]
        right = lax.dynamic_slice_in_dim(lengths, start, span, 0)[None, :]
        amp_right = lax.dynamic_slice_in_dim(amplitude, start, span, 0)[None, :]
        denom = left * left + right * right
        vals = (
            amplitude[:, None]
            * amp_right
            * jnp.sqrt(2.0 * left * right / denom)
            * jnp.exp(-diff * diff / denom)
        )
        return vals.astype(BF16)

    return lax.map(one_block, jnp.arange(count, dtype=jnp.int32))


def data_rows(packed, resp_perm, stud_perm, blocks, order, inverse):
    rows, chans = packed.shape
    nblk, width = (blocks.shape[0], blocks.shape[1])
    moved = jnp.take(packed, order, axis=1).reshape(rows, nblk, width)
    product = jnp.einsum("rbi,bij->rbj", moved, blocks, preferred_element_type=F32).reshape(rows, chans)
    permuted = stud_perm.astype(F32) * (product - resp_perm.astype(F32))
    return jnp.take(permuted, inverse, axis=1).astype(BF16)


def general(gains, response, student, blocks, order, lower, upper, lengths, amplitude):
    nwide = lax.axis_size("wide")
    chd, epochs = gains.shape
    epd = epochs // nwide
    chans = chd * nwide
    inverse = jnp.zeros((chans,), jnp.int32).at[order].set(jnp.arange(chans, dtype=jnp.int32))
    resp_perm = jnp.take(response, order, axis=1)
    stud_perm = jnp.take(student, order, axis=1)
    span = min(256, epochs)
    kernel_stack = covar_stack(lengths, amplitude, span)
    current = gains
    for step in range(ITERS):
        packed = current.astype(BF16).reshape(chd, nwide, epd)
        got = (
            lax.all_to_all(packed, "wide", split_axis=1, concat_axis=0, tiled=True)
            .reshape(chans, epd)
            .T
        )
        misfit_rows = data_rows(got, resp_perm, stud_perm, blocks, order, inverse)
        misfit = lax.all_to_all(
            misfit_rows.T.reshape(chans, 1, epd), "wide", split_axis=0, concat_axis=1, tiled=True
        ).reshape(chd, epochs)
        smoothed = jnp.einsum("ce,bes->cbs", misfit, kernel_stack, preferred_element_type=F32).reshape(
            chd, epochs
        )
        current = jnp.clip(current - 0.02 * smoothed, lower[:, None], upper[:, None])
    return current


def per_device(*args):
    ndev = lax.axis_size("wide")
    chd, epochs = args[0].shape
    fits = ndev >= 8 and ndev & (ndev - 1) == 0 and chd % 128 == 0 and (epochs // ndev) % 256 == 0
    return (fast if fits else general)(*args)


def solution(mesh):
    placed = (
        P(("half", "wide"), None),
        P("wide", "half"),
        P("wide", "half"),
        P("half", None, None),
        P("half"),
        P(("half", "wide")),
        P(("half", "wide")),
        P(),
        P(),
    )
    return jax.shard_map(
        per_device, mesh=mesh, in_specs=placed, out_specs=P(("half", "wide"), None), check_vma=False
    )
```

```python
import math
import jax
import jax.numpy as jnp
from jax import lax
from jax.experimental import pallas as pl
from jax.experimental.pallas import tpu as pltpu
from jax.sharding import PartitionSpec as P

ITERS = 2
LN2 = math.log(2.0)
F32 = jnp.float32
BF16 = jnp.bfloat16


def params(mib=8):
    return pltpu.CompilerParams(vmem_limit_bytes=mib * 1024 * 1024)


CHEAP = pl.CostEstimate(flops=1, bytes_accessed=1, transcendentals=0)
SMEM = pl.BlockSpec(memory_space=pltpu.SMEM)
VMEM = pl.BlockSpec(memory_space=pltpu.VMEM)
HBM = pl.BlockSpec(memory_space=pltpu.HBM)


def dot(a, b):
    return jnp.dot(a, b, preferred_element_type=F32)


def column(row):
    n = row.shape[1]
    return jnp.broadcast_to(row, (n, n)).T[:, :1]


def pack(me, gains, ndev, epd):
    chd, total = gains.shape
    half = ndev // 2
    order = [*range(1, ndev), 0]

    def body(me_ref, gains_ref, *refs):
        outs, kept, sems = refs[:ndev], refs[ndev : ndev + 2], refs[ndev + 2]

        def place(r):
            return kept[r // half].at[:, pl.ds(r % half * epd, epd)]

        def copy(r):
            theirs = pl.ds(pl.multiple_of((me_ref[0] ^ r) * epd, epd), epd)
            return pltpu.make_async_copy(gains_ref.at[:, theirs], place(r), sems.at[r])

        for r in order:
            copy(r).start()
        for r in order:
            copy(r).wait()
            outs[r][...] = place(r)[...].astype(BF16)

    return pl.pallas_call(
        body,
        out_shape=[jax.ShapeDtypeStruct((chd, epd), BF16)] * ndev + [pltpu.VMEM((chd, total // 2), F32)] * 2,
        in_specs=[SMEM, HBM],
        out_specs=[VMEM] * (ndev + 2),
        scratch_shapes=[pltpu.SemaphoreType.DMA((ndev,))],
        compiler_params=params(),
        cost_estimate=CHEAP,
        name="pack_gains",
    )(me, pltpu.with_memory_space_constraint(gains, pltpu.HBM))


def flip(me, data, ndev, factors=None):
    epd, chans = data.shape
    chd = chans // ndev
    kind = BF16 if factors is None else F32
    more = [] if factors is None else [factors]

    def body(me_ref, data_ref, *refs):
        for r in range(ndev):
            cols = pl.ds(pl.multiple_of((me_ref[0] ^ r) * chd, chd), chd)
            out = data_ref[:, cols].astype(F32).T
            if more:
                out = out * refs[0][:, pl.ds(pl.multiple_of(me_ref[0] * epd, epd), epd)]
            refs[-1][pl.ds(r * chd, chd), :] = out.astype(kind)

    return pl.pallas_call(
        body,
        out_shape=pltpu.VMEM((chans, epd), kind),
        in_specs=[SMEM, VMEM] + [VMEM] * len(more),
        out_specs=VMEM,
        compiler_params=params(),
        cost_estimate=CHEAP,
        name="flip",
    )(me, data, *more)


def dense(me, blocks, channels, ndev):
    nblk, width, _ = blocks.shape
    chans = nblk * width
    chd = chans // ndev

    def body(me_ref, blocks_ref, order_ref, out_ref, left_ref, hot_ref):
        def names_along(dim, shape):
            at = lax.broadcasted_iota(jnp.int32, shape, dim)
            return (((at // chd) ^ me_ref[0]) * chd + at % chd).astype(F32)

        down = names_along(0, (chans, width))
        along = names_along(1, (width, chans))
        for b in range(nblk):
            span = pl.ds(b * width, width)
            names = order_ref[:, span].astype(F32)
            hot = jnp.where(down == names, 1.0, 0.0).astype(BF16)
            left_ref[:, span] = dot(hot, blocks_ref[b]).astype(BF16)
            hot_ref[span, :] = jnp.where(along == column(names), 1.0, 0.0).astype(BF16)
        for r in range(0, chans, width):
            rows, rest = pl.ds(r, width), pl.ds(r, chans - r)
            tile = dot(left_ref[rows, :], hot_ref[:, rest]).astype(BF16)
            out_ref[rows, rest] = tile
            for c in range(r + width, chans, width):
                out_ref[pl.ds(c, width), rows] = tile[:, c - r : c - r + width].T

    return pl.pallas_call(
        body,
        out_shape=pltpu.VMEM((chans, chans), BF16),
        in_specs=[SMEM, VMEM, VMEM],
        out_specs=VMEM,
        scratch_shapes=[pltpu.VMEM((chans, chans), BF16)] * 2,
        compiler_params=params(),
        cost_estimate=CHEAP,
        name="dense_blocks",
    )(me, blocks, channels[None, :])


def distances(total):
    def body(out_ref):
        row = lax.broadcasted_iota(jnp.int32, (128, 128), 0)
        away = (row - lax.broadcasted_iota(jnp.int32, (128, 128), 1)).astype(F32)
        back = -away
        for c in range(0, 2 * total, 128):
            out_ref[:, pl.ds(c, 128)] = (away + float(total - c)) * (back - float(total - c))

    return pl.pallas_call(
        body,
        out_shape=pltpu.VMEM((128, 2 * total), F32),
        out_specs=VMEM,
        compiler_params=params(),
        cost_estimate=CHEAP,
        name="distances",
    )()


def covar_tiles(me_ref, away_ref, squares_ref, own_ref, offset, k, others, epd, store):
    group = 32
    total = squares_ref.shape[1]
    base = (me_ref[0] ^ offset) * epd + k * 128
    span = pl.ds(pl.multiple_of(base, 128), 128)
    own_ref[...] = jnp.broadcast_to(squares_ref[:, span], (128, 128)).T
    for r in others:
        first = (me_ref[0] ^ r) * epd
        for c in range(0, epd, 128):
            theirs = squares_ref[:, pl.ds(pl.multiple_of(first + c, 128), 128)]
            window = pl.ds(pl.multiple_of(total + first + c - base, 128), 128)
            parts = []
            for g in range(0, 128, group):
                rows = pl.ds(g, group)
                q = lax.rsqrt(own_ref[rows, :] + theirs)
                parts.append((q * jnp.exp2(away_ref[rows, window] * (q * q))).astype(BF16))
            store(r, c, jnp.concatenate(parts, axis=0))


def covar_own(me, away, squares, offsets, epd):
    per = epd // 128
    first = offsets[0]
    count = len(offsets) * epd

    def body(me_ref, away_ref, squares_ref, out_ref, own_ref):
        for n, offset in enumerate(offsets):

            def block(k, _):
                mine = pl.ds(pl.multiple_of(n * epd + k * 128, 128), 128)

                def store(r, c, tile):
                    theirs = pl.ds((r - first) * epd + c, 128)
                    out_ref[mine, theirs] = tile
                    if r != offset:
                        out_ref[theirs, mine] = tile.T

                covar_tiles(me_ref, away_ref, squares_ref, own_ref, offset, k, offsets[n:], epd, store)
                return 0

            lax.fori_loop(0, per, block, 0)

    return pl.pallas_call(
        body,
        out_shape=pltpu.VMEM((count, count), BF16),
        in_specs=[SMEM, VMEM, VMEM],
        out_specs=VMEM,
        scratch_shapes=[pltpu.VMEM((128, 128), F32)],
        compiler_params=params(),
        cost_estimate=CHEAP,
        name="covar_own",
    )(me, away, squares)


def covar_cross(me, away, squares, near, far, epd):
    per = epd // 128
    shape = (len(near) * epd, len(far) * epd)

    def body(me_ref, away_ref, squares_ref, out_ref, flip_ref, own_ref):
        def block(n, _):
            mine = pl.ds(pl.multiple_of(n * 128, 128), 128)

            def store(r, c, tile):
                theirs = pl.ds((r - far[0]) * epd + c, 128)
                out_ref[mine, theirs] = tile
                flip_ref[theirs, mine] = tile.T

            covar_tiles(me_ref, away_ref, squares_ref, own_ref, near[0] + n // per, n % per, far, epd, store)
            return 0

        lax.fori_loop(0, shape[0] // 128, block, 0)

    return pl.pallas_call(
        body,
        out_shape=[pltpu.VMEM(shape, BF16), pltpu.VMEM(shape[::-1], BF16)],
        in_specs=[SMEM, VMEM, VMEM],
        out_specs=[VMEM] * 2,
        scratch_shapes=[pltpu.VMEM((128, 128), F32)],
        compiler_params=params(),
        cost_estimate=CHEAP,
        name="covar_cross",
    )(me, away, squares)


def normal(weights, pieces, resp, stud, order):
    ndev = len(pieces)
    chd, epd = pieces[0].shape
    chans = ndev * chd

    def body(*refs):
        ins, (w_ref, resp_ref, stud_ref), outs, got = refs[:ndev], refs[ndev : ndev + 3], refs[ndev + 3 : -1], refs[-1]
        for r, ref in zip([*order, 0], ins):
            got[pl.ds(r * chd, chd), :] = ref[...]
        for r in range(ndev):
            rows = pl.ds(r * chd, chd)
            product = dot(w_ref[rows, :], got[...])
            outs[r][...] = (stud_ref[rows, :] * (product - resp_ref[rows, :].astype(F32))).astype(BF16)

    return list(
        pl.pallas_call(
            body,
            out_shape=[jax.ShapeDtypeStruct((chd, epd), BF16)] * ndev,
            in_specs=[VMEM] * (3 + ndev),
            out_specs=[VMEM] * ndev,
            scratch_shapes=[pltpu.VMEM((chans, epd), BF16)],
            compiler_params=params(),
            cost_estimate=CHEAP,
            name="normal_step",
        )(*[pieces[r] for r in [*order, 0]], weights, resp, stud)
    )


def terms_of(offsets, half):
    runs = []
    for r in sorted(offsets):
        if runs and runs[-1][1][-1] == r - 1 and r != half:
            runs[-1][1].append(r)
        else:
            runs.append((r // half, [r], r % half))
    return runs


def sides_of(offsets, half):
    return sorted({r // half for r in offsets})


def products(got, offsets, rows, refs):
    half = len(got) // 2
    epd = got[0].shape[1]
    pieces = {r: next(refs) for r in offsets}
    sides = {side: [next(refs) for _ in rows[side]] for side in sides_of(offsets, half)}
    return [
        (
            jnp.concatenate([pieces[r][...] for r in run], axis=1),
            sides[side],
            pl.ds(at * epd, len(run) * epd),
        )
        for side, run, at in terms_of(offsets, half)
    ]


def partial(got, offsets, rows, before):
    chd, epd = got[0].shape
    span = max(block.shape[1] for side in rows for block in side)
    blocks = max(len(side) for side in rows)
    args = [got[r] for r in offsets] + [block for side in sides_of(offsets, len(got) // 2) for block in rows[side]]
    more = [] if before is None else [before]

    def body(*refs):
        given = iter(refs)
        terms = products(got, offsets, rows, given)
        before_ref, out_ref = [next(given) for _ in more], refs[-1]
        for b in range(blocks):
            for c in range(0, span, epd):
                cols = pl.ds(b * span + c, epd)
                acc = before_ref[0][:, cols] if more else None
                for left, side, at in terms:
                    term = dot(left, side[b][at, pl.ds(c, epd)])
                    acc = term if acc is None else acc + term
                out_ref[:, cols] = acc

    return pl.pallas_call(
        body,
        out_shape=pltpu.VMEM((chd, blocks * span), F32),
        in_specs=[VMEM] * (len(args) + len(more)),
        out_specs=VMEM,
        compiler_params=params(),
        cost_estimate=CHEAP,
        name="smooth_part",
    )(*args, *more)


def update(me, got, offsets, rows, before, current, factors, lower, upper, last):
    chd, epd = got[0].shape
    ndev = len(got)
    total = ndev * epd
    wide = current[0].shape[1]
    span = max(block.shape[1] for side in rows for block in side)
    args = [got[r] for r in offsets] + [block for side in sides_of(offsets, len(got) // 2) for block in rows[side]]

    def body(me_ref, *refs):
        given = iter(refs)
        terms = products(got, offsets, rows, given)
        before_ref = next(given)
        cur_refs = [next(given) for _ in current]
        factors_ref, low, high = next(given), column(next(given)[...]), column(next(given)[...])
        outs = list(given)
        copies = []
        for n in range(ndev):
            cols = pl.ds(n * epd, epd)
            block, c = divmod(n * epd, span)
            acc = before_ref[:, cols]
            for left, side, at in terms:
                acc = acc + dot(left, side[block][at, pl.ds(c, epd)])
            theirs = pl.ds(pl.multiple_of((me_ref[0] ^ n) * epd, epd), epd)
            gone = acc * (0.02 * factors_ref[:, theirs])
            new = jnp.clip(cur_refs[n * epd // wide][:, pl.ds(n * epd % wide, epd)] - gone, low, high)
            if last:
                out_ref, stage, sems = outs
                stage[:, cols] = new
                copies.append(pltpu.make_async_copy(stage.at[:, cols], out_ref.at[:, theirs], sems.at[n]))
                copies[-1].start()
            else:
                outs[0][:, cols] = new
                outs[1 + n][...] = new.astype(BF16)
        for copy in copies:
            copy.wait()

    if last:
        shapes, specs = [jax.ShapeDtypeStruct((chd, total), F32)], [HBM]
        scratch = [pltpu.VMEM((chd, total), F32), pltpu.SemaphoreType.DMA((ndev,))]
    else:
        shapes = [pltpu.VMEM((chd, total), F32)] + [jax.ShapeDtypeStruct((chd, epd), BF16)] * ndev
        specs, scratch = [VMEM] * (1 + ndev), []
    out, *pieces = pl.pallas_call(
        body,
        out_shape=shapes,
        in_specs=[SMEM] + [VMEM] * (len(args) + len(current) + 4),
        out_specs=specs,
        scratch_shapes=scratch,
        compiler_params=params(),
        cost_estimate=CHEAP,
        name="update",
    )(me, *args, before, *current, factors, lower, upper)
    return out, pieces


def swap(pieces):
    ndev = len(pieces)
    return [pieces[0]] + [
        lax.ppermute(pieces[r], "wide", [(i, i ^ r) for i in range(ndev)]) for r in range(1, ndev)
    ]


def fast(gains, response, student, blocks, channels, lower, upper, lengths, amplitude):
    ndev = lax.axis_size("wide")
    epd = gains.shape[1] // ndev
    half = ndev // 2
    near, far = list(range(half)), list(range(half, ndev))
    me = lax.axis_index("wide").astype(jnp.int32).reshape(1)
    low, high = lower[None, :], upper[None, :]
    squares = (lengths * lengths * LN2)[None, :]
    factors = (amplitude * jnp.sqrt(lengths * math.sqrt(2.0 * LN2)))[None, :]
    tied = lax.optimization_barrier

    order = [*far[half // 2 :], *near[1:], *far[: half // 2]]
    groups = [far[:1], near, far[1:-1]]
    latest = far[-1:]

    *packed, kept_near, kept_far = pack(me, gains, ndev, epd)
    got = swap(packed)
    weights = dense(me, blocks, channels, ndev)
    resp = flip(me, response, ndev)
    stud = flip(me, student, ndev, factors)
    away = distances(gains.shape[1])
    near_far, far_near = covar_cross(me, away, squares, near, far, epd)
    arrived, near_far, far_near = tied(([got[r] for r in order], near_far, far_near))
    got = {0: got[0], **dict(zip(order, arrived))}

    misfit = normal(weights, got, resp, stud, order)
    part, misfit = tied((squares, misfit))
    far_far = covar_own(me, away, part, far, epd)
    misfit[-1], far_far = tied((misfit[-1], far_far))
    near_near = covar_own(me, away, squares, near, epd)
    misfit[0], near_near = tied((misfit[0], near_near))
    got = swap(misfit)
    rows = [[near_near, near_far], [far_near, far_far]]
    total = None
    for group in groups:
        total = partial(got, group, rows, total)
    current = [kept_near, kept_far]
    current, packed = update(me, got, latest, rows, total, current, factors, low, high, False)

    got = swap(normal(weights, swap(packed), resp, stud, order))
    total = None
    for group in groups:
        total = partial(got, group, rows, total)
    out, _ = update(me, got, latest, rows, total, [current], factors, low, high, True)
    return out


def covar_stack(lengths, amplitude, span):
    total = lengths.shape[0]
    count = total // span
    rows = jnp.arange(total, dtype=jnp.int32)

    def one_block(index):
        start = index * span
        cols = start + jnp.arange(span, dtype=jnp.int32)
        diff = (rows[:, None] - cols[None, :]).astype(lengths.dtype)
        left = lengths[:, None]
        right = lax.dynamic_slice_in_dim(lengths, start, span, 0)[None, :]
        amp_right = lax.dynamic_slice_in_dim(amplitude, start, span, 0)[None, :]
        denom = left * left + right * right
        vals = (
            amplitude[:, None]
            * amp_right
            * jnp.sqrt(2.0 * left * right / denom)
            * jnp.exp(-diff * diff / denom)
        )
        return vals.astype(BF16)

    return lax.map(one_block, jnp.arange(count, dtype=jnp.int32))


def data_rows(packed, resp_perm, stud_perm, blocks, order, inverse):
    rows, chans = packed.shape
    nblk, width = (blocks.shape[0], blocks.shape[1])
    moved = jnp.take(packed, order, axis=1).reshape(rows, nblk, width)
    product = jnp.einsum("rbi,bij->rbj", moved, blocks, preferred_element_type=F32).reshape(rows, chans)
    permuted = stud_perm.astype(F32) * (product - resp_perm.astype(F32))
    return jnp.take(permuted, inverse, axis=1).astype(BF16)


def general(gains, response, student, blocks, order, lower, upper, lengths, amplitude):
    nwide = lax.axis_size("wide")
    chd, epochs = gains.shape
    epd = epochs // nwide
    chans = chd * nwide
    inverse = jnp.zeros((chans,), jnp.int32).at[order].set(jnp.arange(chans, dtype=jnp.int32))
    resp_perm = jnp.take(response, order, axis=1)
    stud_perm = jnp.take(student, order, axis=1)
    span = min(256, epochs)
    kernel_stack = covar_stack(lengths, amplitude, span)
    current = gains
    for step in range(ITERS):
        packed = current.astype(BF16).reshape(chd, nwide, epd)
        got = (
            lax.all_to_all(packed, "wide", split_axis=1, concat_axis=0, tiled=True)
            .reshape(chans, epd)
            .T
        )
        misfit_rows = data_rows(got, resp_perm, stud_perm, blocks, order, inverse)
        misfit = lax.all_to_all(
            misfit_rows.T.reshape(chans, 1, epd), "wide", split_axis=0, concat_axis=1, tiled=True
        ).reshape(chd, epochs)
        smoothed = jnp.einsum("ce,bes->cbs", misfit, kernel_stack, preferred_element_type=F32).reshape(
            chd, epochs
        )
        current = jnp.clip(current - 0.02 * smoothed, lower[:, None], upper[:, None])
    return current


def per_device(*args):
    ndev = lax.axis_size("wide")
    chd, epochs = args[0].shape
    fits = ndev >= 8 and ndev & (ndev - 1) == 0 and chd % 128 == 0 and (epochs // ndev) % 256 == 0
    return (fast if fits else general)(*args)


def solution(mesh):
    placed = (
        P(("half", "wide"), None),
        P("wide", "half"),
        P("wide", "half"),
        P("half", None, None),
        P("half"),
        P(("half", "wide")),
        P(("half", "wide")),
        P(),
        P(),
    )
    return jax.shard_map(
        per_device, mesh=mesh, in_specs=placed, out_specs=P(("half", "wide"), None), check_vma=False
    )
```
